32 devices in a mesh: groups: 2 (over y), ax: 4 (over z), az: 2 (over x), rad: 2 (over core).
Axes of the slice: x: 2, y: 2, z: 4, core: 2. Of those that a mesh axis runs over, the one named last changes fastest.
Arguments:
- flow_state: float32 [4, 16, 96, 256], P(None, ('groups', 'ax'), 'rad', 'az'), parts along dimension 1, may hold values from -2 to 2, as said below
- cycle_widths: int32 [8], replicated, may hold values from 2 to 256, as said below
Outputs:
- advanced: float32 [4, 16, 96, 256], P(None, ('groups', 'ax'), 'rad', 'az'), parts along dimension 1
The draws below stay inside these ranges and needn't reach their ends.
There are 2 independent parts, one for each index of `groups`. The reference program is written for one: setup_inputs(seed, part) draws one part's arguments, and reference() takes and returns one part's arrays. A program takes and returns all parts, laid end to end along the dimension named above; an argument that names none is the same for every part. Nothing has to cross between parts.
Inputs may be any that keep to these rules, and one draw needn't show every extreme that they name: `flow_state`: channel 0 lies in 0 to 1. `cycle_widths`: each entry is a power of two that divides 256; entry 0 equals 256.
All inputs are finite; a program needn't handle non-finite values.
Results may differ from the reference program's by a relative error of at most 0.0003.
Values sent between devices are 32-bit elements; how exact they have to be, the bound alone decides.
A program may use at most 64 MiB of HBM per device.

```python
import math
import jax
import jax.numpy as jnp
from jax import lax

STEPS = 2
NA = 8
NR = 96
NT = 256
NRING = 8


def draw_flow_state(key, part):
    key = jax.random.fold_in(key, 1)
    level_key, motion_key = jax.random.split(key)
    level_set = jax.random.uniform(level_key, (1, NA, NR, NT), jnp.float32)
    motion = jnp.clip(0.5 * jax.random.normal(motion_key, (3, NA, NR, NT), jnp.float32), -2.0, 2.0)
    return jnp.concatenate([level_set, motion], 0)


def draw_cycle_widths(key, part):
    key = jax.random.fold_in(key, 2)
    levels = NT.bit_length() - 1
    cycle_index = jnp.arange(NRING, dtype=jnp.int32)
    shift_count = jax.random.randint(key, (NRING,), 1, levels, dtype=jnp.int32)
    shift_count = jnp.where(cycle_index == 0, 0, shift_count)
    return jnp.right_shift(jnp.int32(NT), shift_count)


def setup_inputs(seed: int = 0, part: int = 0) -> dict:
    keys = jax.random.split(jax.random.key(seed), 3)
    own_keys = jax.random.split(jax.random.fold_in(keys[2], part), 3)
    return {
        "flow_state": draw_flow_state(jax.random.fold_in(jax.random.fold_in(keys[2], part), 71), part),
        "cycle_widths": draw_cycle_widths(jax.random.fold_in(keys[2], 71), part),
    }


DT = 0.2
KAPPA = 0.05
VISC = 0.1
RHO_RATIO = 20.0


def rates(center, upper_plane, lower_plane, outer_cycle, inner_cycle, ahead_cell, behind_cell, radius, angle_step):
    level_set = center[0]
    axial_speed = center[1]
    radial_speed = center[2]
    swirl_speed = center[3]
    reciprocal = 1.0 / radius
    arc_scale = 1.0 / (2.0 * radius * angle_step)
    level_flux = (upper_plane[1] * upper_plane[0] - lower_plane[1] * lower_plane[0]) * 0.5
    level_flux = level_flux + ((radius + 1.0) * outer_cycle[2] * outer_cycle[0] - (radius - 1.0) * inner_cycle[2] * inner_cycle[0]) * 0.5 * reciprocal
    level_flux = level_flux + (ahead_cell[3] * ahead_cell[0] - behind_cell[3] * behind_cell[0]) * arc_scale
    diffused = upper_plane + lower_plane - 2.0 * center + ((radius + 0.5) * (outer_cycle - center) - (radius - 0.5) * (center - inner_cycle)) * reciprocal
    level_rate = -level_flux + KAPPA * diffused[0]
    density = 1.0 + (RHO_RATIO - 1.0) * jnp.clip(level_set, 0.0, 1.0)
    transport = axial_speed * (upper_plane[1:] - lower_plane[1:]) * 0.5
    transport = transport + radial_speed * (outer_cycle[1:] - inner_cycle[1:]) * 0.5
    transport = transport + swirl_speed * (ahead_cell[1:] - behind_cell[1:]) * arc_scale
    viscous = VISC / density * diffused[1:]
    curvature = jnp.stack([jnp.zeros_like(level_set), swirl_speed * swirl_speed * reciprocal, -swirl_speed * radial_speed * reciprocal])
    velocity_rates = -transport + viscous + curvature
    return DT * jnp.concatenate([level_rate[None], velocity_rates], 0)


def coarsen(packed):
    values, cycle_width = packed
    column = jnp.arange(NT, dtype=jnp.int32)
    same_block = (column[:, None] // cycle_width) == (column[None, :] // cycle_width)
    average = same_block.astype(values.dtype) / cycle_width.astype(values.dtype)
    flattened = values.reshape(-1, NT)
    return jnp.dot(flattened, average, precision=lax.Precision.HIGHEST).reshape(values.shape)


def advance(current, cycle_widths):
    angle_step = 2.0 * math.pi / NT
    radius = (jnp.arange(NR, dtype=jnp.int32).astype(current.dtype) + 0.5)[:, None]
    mirror = jnp.array([1.0, 1.0, -1.0, -1.0], current.dtype)[:, None, None]
    opposite = jnp.roll(current[:, :, 0, :], NT // 2, axis=2) * mirror
    zero_row = jnp.zeros_like(current[:, :, :1, :])
    radial_ext = jnp.concatenate([opposite[:, :, None, :], current, zero_row], axis=2)
    axial_ext = jnp.pad(current, ((0, 0), (1, 1), (0, 0), (0, 0)))
    increment = rates(current, axial_ext[:, 2:], axial_ext[:, :-2], radial_ext[:, :, 2:], radial_ext[:, :, :-2],
                      jnp.roll(current, -1, axis=3), jnp.roll(current, 1, axis=3), radius, angle_step)
    cycle_head = jnp.moveaxis(increment[:, :, :NRING, :], 2, 0)
    coarse = lax.map(coarsen, (cycle_head, cycle_widths))
    cycle_head = jnp.moveaxis(coarse, 0, 2)
    increment = jnp.concatenate([cycle_head, increment[:, :, NRING:]], axis=2)
    return current + increment


def reference(flow_state, cycle_widths):
    current = flow_state
    for repeat in range(STEPS):
        current = advance(current, cycle_widths)
    return current
```

```python
import functools
import math

import jax
import jax.numpy as jnp
from jax import lax
from jax.experimental import pallas as pl
from jax.experimental.pallas import tpu as pltpu
from jax.sharding import PartitionSpec as P

STEPS = 2
DT = 0.2
KAPPA = 0.05
VISC = 0.1
RHO_RATIO = 20.0
PAD = 8
MESH = pl.DeviceIdType.MESH


def kernel(
    sizes,
    bounds,
    flow_ref,
    width_ref,
    out_ref,
    state,
    increment,
    spread,
    low_plane,
    high_plane,
    edge_out,
    edge_left,
    edge_right,
    row_out,
    row_in,
    sum_out,
    sum_in,
    load_sem,
    low_send,
    low_recv,
    high_send,
    high_recv,
    left_send,
    left_recv,
    right_send,
    right_recv,
    row_send,
    row_recv,
    opposite_send,
    opposite_recv,
    sum_send,
    sum_recv,
):
    axials, sectors, rads = sizes
    channels, planes, rows, columns = flow_ref.shape
    blocks = channels * planes
    rings = width_ref.shape[0]
    chunks = len(bounds) - 1
    ax = lax.axis_index("ax")
    az = lax.axis_index("az")
    rad = lax.axis_index("rad")
    angle_step = 2.0 * math.pi / (sectors * columns)
    half_arc = DT / (2.0 * angle_step)
    has_low = ax > 0
    has_high = ax < axials - 1
    has_inner = rad > 0
    has_outer = rad < rads - 1
    at_axis = rad == 0
    left = (az + sectors - 1) % sectors
    right = (az + 1) % sectors
    partner = (az + sectors // 2) % sectors

    load = pltpu.make_async_copy(
        flow_ref, state.at[0, :, :, pl.ds(PAD, rows)], load_sem
    )
    load.start()

    barrier = pltpu.get_barrier_semaphore()

    def greet(axis, place):
        pl.semaphore_signal(barrier, inc=1, device_id={axis: place}, device_id_type=MESH)

    @pl.when(has_low)
    def _():
        greet("ax", ax - 1)

    @pl.when(has_high)
    def _():
        greet("ax", ax + 1)

    @pl.when(has_inner)
    def _():
        greet("rad", rad - 1)

    @pl.when(has_outer)
    def _():
        greet("rad", rad + 1)

    for shift in range(1, sectors):
        greet("az", (az + shift) % sectors)

    def one(flag):
        return jnp.where(flag, 1, 0)

    pl.semaphore_wait(
        barrier,
        one(has_low) + one(has_high) + one(has_inner) + one(has_outer) + sectors - 1,
    )

    def remote(src, dst, send, recv, axis, place):
        return pltpu.make_async_remote_copy(
            src_ref=src,
            dst_ref=dst,
            send_sem=send,
            recv_sem=recv,
            device_id={axis: place},
            device_id_type=MESH,
        )

    def span(chunk):
        return pl.ds(bounds[chunk], bounds[chunk + 1] - bounds[chunk])

    def own(chunk):
        return pl.ds(PAD + bounds[chunk], bounds[chunk + 1] - bounds[chunk])

    def source(step, plane, chunk):
        if step == 0:
            return flow_ref.at[:, plane, span(chunk)]
        return state.at[step, :, plane, own(chunk)]

    def to_low(step, chunk):
        return remote(
            source(step, 0, chunk),
            high_plane.at[step, :, span(chunk)],
            low_send.at[step, chunk],
            low_recv.at[step, chunk],
            "ax",
            ax - 1,
        )

    def to_high(step, chunk):
        return remote(
            source(step, planes - 1, chunk),
            low_plane.at[step, :, span(chunk)],
            high_send.at[step, chunk],
            high_recv.at[step, chunk],
            "ax",
            ax + 1,
        )

    def to_right(step, chunk):
        return remote(
            edge_out.at[step, span(chunk)],
            edge_left.at[step, span(chunk)],
            right_send.at[step, chunk],
            right_recv.at[step, chunk],
            "az",
            right,
        )

    def to_left(step, chunk):
        return remote(
            edge_out.at[step, span(chunk)],
            edge_right.at[step, span(chunk)],
            left_send.at[step, chunk],
            left_recv.at[step, chunk],
            "az",
            left,
        )

    def to_inner(step):
        return remote(
            row_out.at[step, 0],
            row_in.at[step, 1],
            row_send.at[step, 0],
            row_recv.at[step, 0],
            "rad",
            rad - 1,
        )

    def to_outer(step):
        return remote(
            row_out.at[step, 1],
            row_in.at[step, 0],
            row_send.at[step, 1],
            row_recv.at[step, 1],
            "rad",
            rad + 1,
        )

    def to_opposite(step):
        return remote(
            row_out.at[step, 0],
            row_in.at[step, 0],
            opposite_send.at[step],
            opposite_recv.at[step],
            "az",
            partner,
        )

    def to_sector(step, shift):
        return remote(
            sum_out.at[step],
            sum_in.at[step, shift - 1],
            sum_send.at[step, shift - 1],
            sum_recv.at[step, shift - 1],
            "az",
            (az + shift) % sectors,
        )

    def send_planes(step, chunk):
        @pl.when(has_low)
        def _():
            to_low(step, chunk).start()

        @pl.when(has_high)
        def _():
            to_high(step, chunk).start()

    def send_edges(step, chunk):
        count = bounds[chunk + 1] - bounds[chunk]
        lane = lax.broadcasted_iota(jnp.int32, (count, columns), 1)
        packed = jnp.zeros((count, columns), jnp.float32)
        for block in range(blocks):
            values = state[step, block // planes, block % planes, own(chunk)]
            packed = jnp.where(
                lane // 2 == block, pltpu.roll(values, 2 * block + 1, 1), packed
            )
        edge_out[step, span(chunk)] = packed
        to_right(step, chunk).start()
        if sectors > 2:
            to_left(step, chunk).start()

    def send_first_row(step):
        for block in range(blocks):
            row_out[step, 0, pl.ds(block, 1)] = state[
                step, block // planes, block % planes, pl.ds(PAD, 1)
            ]

        @pl.when(has_inner)
        def _():
            to_inner(step).start()

        @pl.when(at_axis)
        def _():
            to_opposite(step).start()

    def send_last_row(step):
        for block in range(blocks):
            row_out[step, 1, pl.ds(block, 1)] = state[
                step, block // planes, block % planes, pl.ds(PAD + rows - 1, 1)
            ]

        @pl.when(has_outer)
        def _():
            to_outer(step).start()

    def receive_rows(step):
        @pl.when(has_inner)
        def _():
            to_outer(step).wait_recv()
            for block in range(blocks):
                state[step, block // planes, block % planes, pl.ds(PAD - 1, 1)] = row_in[
                    step, 0, pl.ds(block, 1)
                ]

        @pl.when(at_axis)
        def _():
            to_opposite(step).wait_recv()
            for block in range(blocks):
                sign = 1.0 if block // planes < 2 else -1.0
                state[step, block // planes, block % planes, pl.ds(PAD - 1, 1)] = (
                    sign * row_in[step, 0, pl.ds(block, 1)]
                )

        @pl.when(has_outer)
        def _():
            to_inner(step).wait_recv()
            for block in range(blocks):
                state[step, block // planes, block % planes, pl.ds(PAD + rows, 1)] = row_in[
                    step, 1, pl.ds(block, 1)
                ]

        @pl.when(jnp.logical_not(has_outer))
        def _():
            for block in range(blocks):
                state[step, block // planes, block % planes, pl.ds(PAD + rows, 1)] = jnp.zeros(
                    (1, columns), jnp.float32
                )

    def in_plane(step, chunk):
        to_right(step, chunk).wait_recv()
        if sectors > 2:
            to_left(step, chunk).wait_recv()
        for start in range(bounds[chunk], bounds[chunk + 1], 8):
            shape = (8, columns)
            lane = lax.broadcasted_iota(jnp.int32, shape, 1)
            row = lax.broadcasted_iota(jnp.int32, shape, 0)
            radius = (rad * rows + start + row).astype(jnp.float32) + 0.5
            reciprocal = 1.0 / radius
            arc = half_arc * reciprocal
            outer_weight = 1.0 + 0.5 * reciprocal
            inner_weight = 1.0 - 0.5 * reciprocal
            outer_flux = (0.5 * DT) * (1.0 + reciprocal)
            inner_flux = (0.5 * DT) * (1.0 - reciprocal)
            edges = edge_left[step, pl.ds(start, 8)]
            if sectors > 2:
                edges = jnp.where(lane % 2 == 0, edges, edge_right[step, pl.ds(start, 8)])

            def cell(channel, plane, offset=0):
                return state[step, channel, plane, pl.ds(PAD + start + offset, 8)]

            for plane in range(planes):
                center = [cell(c, plane) for c in range(channels)]
                outer = [cell(c, plane, 1) for c in range(channels)]
                inner = [cell(c, plane, -1) for c in range(channels)]
                ahead, behind = [], []
                for c in range(channels):
                    block = c * planes + plane
                    rim = pltpu.roll(edges, (columns - 2 * block - 1) % columns, 1)
                    ahead.append(
                        pltpu.roll(jnp.where(lane == 0, rim, center[c]), columns - 1, 1)
                    )
                    behind.append(
                        pltpu.roll(jnp.where(lane == columns - 1, rim, center[c]), 1, 1)
                    )
                level, axial, radial, swirl = center
                density = 1.0 + (RHO_RATIO - 1.0) * jnp.clip(level, 0.0, 1.0)
                thin = (DT * VISC) / density
                spread[plane, pl.ds(start, 8)] = thin
                laplace = [
                    outer_weight * outer[c] + inner_weight * inner[c] - 4.0 * center[c]
                    for c in range(channels)
                ]
                upper = lower = None
                if plane < planes - 1:
                    upper = [cell(c, plane + 1) for c in range(channels)]
                    laplace = [laplace[c] + upper[c] for c in range(channels)]
                if plane > 0:
                    lower = [cell(c, plane - 1) for c in range(channels)]
                    laplace = [laplace[c] + lower[c] for c in range(channels)]
                rate = (
                    (DT * KAPPA) * laplace[0]
                    - outer_flux * outer[2] * outer[0]
                    + inner_flux * inner[2] * inner[0]
                    - arc * (ahead[3] * ahead[0] - behind[3] * behind[0])
                )
                if upper is not None:
                    rate = rate - (0.5 * DT) * upper[1] * upper[0]
                if lower is not None:
                    rate = rate + (0.5 * DT) * lower[1] * lower[0]
                increment[0, plane, pl.ds(start, 8)] = rate
                drift = (0.5 * DT) * axial
                push = (0.5 * DT) * radial
                turn = arc * swirl
                for c in range(1, channels):
                    rate = (
                        thin * laplace[c]
                        - push * (outer[c] - inner[c])
                        - turn * (ahead[c] - behind[c])
                    )
                    if upper is not None:
                        rate = rate - drift * upper[c]
                    if lower is not None:
                        rate = rate + drift * lower[c]
                    if c == 2:
                        rate = rate + (DT * reciprocal) * swirl * swirl
                    if c == 3:
                        rate = rate - (DT * reciprocal) * swirl * radial
                    increment[c, plane, pl.ds(start, 8)] = rate

    def receive_planes(step, chunk):
        @pl.when(has_low)
        def _():
            to_high(step, chunk).wait_recv()

        @pl.when(has_high)
        def _():
            to_low(step, chunk).wait_recv()

    def add_planes(step, chunk):
        for plane, halo, sign in ((0, low_plane, 1.0), (planes - 1, high_plane, -1.0)):
            here = span(chunk)
            drift = (sign * 0.5 * DT) * state[step, 1, plane, own(chunk)]
            weight = drift + spread[plane, here]
            level = halo[step, 0, here]
            increment[0, plane, here] += level * (
                DT * KAPPA + (sign * 0.5 * DT) * halo[step, 1, here]
            )
            for c in range(1, channels):
                increment[c, plane, here] += weight * halo[step, c, here]

    def store(step, chunk):
        for c in range(channels):
            for plane in range(planes):
                value = state[step, c, plane, own(chunk)] + increment[c, plane, span(chunk)]
                if step == STEPS - 1:
                    out_ref[c, plane, span(chunk)] = value
                else:
                    state[step + 1, c, plane, own(chunk)] = value

    def widths(lane_shape):
        row = lax.broadcasted_iota(jnp.int32, lane_shape, 0)
        width = jnp.zeros(lane_shape, jnp.int32)
        for ring in range(rings):
            width = jnp.where(row == ring, width_ref[ring], width)
        return width

    def block_sums(step):
        shape = (rings, columns)
        lane = lax.broadcasted_iota(jnp.int32, shape, 1)
        width = widths(shape)
        values = [
            increment[block // planes, block % planes, pl.ds(0, rings)]
            for block in range(blocks)
        ]
        reach = 1
        while reach < columns:
            high_side = (lane // reach) % 2 == 1
            wide = width > reach
            values = [
                jnp.where(
                    wide,
                    value
                    + jnp.where(
                        high_side,
                        pltpu.roll(value, reach, 1),
                        pltpu.roll(value, columns - reach, 1),
                    ),
                    value,
                )
                for value in values
            ]
            reach *= 2
        packed = jnp.zeros(shape, jnp.float32)
        for block in range(blocks):
            increment[block // planes, block % planes, pl.ds(0, rings)] = values[block]
            packed = jnp.where(lane == block, values[block], packed)
        sum_out[step] = packed
        for shift in range(1, sectors):
            to_sector(step, shift).start()

    def block_means(step):
        shape = (rings, columns)
        width = widths(shape)
        far = jnp.zeros(shape, jnp.float32)
        for shift in range(1, sectors):
            to_sector(step, shift).wait_recv()
            sender = (az + sectors - shift) % sectors
            share = jnp.zeros(shape, jnp.float32)
            size = 2
            while size <= sectors:
                same = jnp.where(sender // size == az // size, 1.0, 0.0)
                share = jnp.where(width == size * columns, same, share)
                size *= 2
            far = far + share * sum_in[step, shift - 1]
        inverse = 1.0 / width.astype(jnp.float32)
        for block in range(blocks):
            here = (block // planes, block % planes, pl.ds(0, rings))
            total = increment[here] + jnp.broadcast_to(far[:, block : block + 1], shape)
            increment[here] = total * inverse

    for chunk in range(chunks):
        send_planes(0, chunk)
    for step in range(STEPS):

        @pl.when(jnp.logical_not(has_low))
        def _():
            low_plane[step] = jnp.zeros(low_plane.shape[1:], jnp.float32)

        @pl.when(jnp.logical_not(has_high))
        def _():
            high_plane[step] = jnp.zeros(high_plane.shape[1:], jnp.float32)

    load.wait()
    send_first_row(0)
    send_last_row(0)
    for chunk in range(chunks):
        send_edges(0, chunk)
    for step in range(STEPS):
        last = step == STEPS - 1
        receive_rows(step)
        for chunk in range(chunks):
            in_plane(step, chunk)
        order = range(chunks) if step == 0 else list(range(1, chunks)) + [0]

        def finish(chunk):
            store(step, chunk)
            if not last:
                send_planes(step + 1, chunk)
                send_edges(step + 1, chunk)
                if chunk == 0:
                    send_first_row(step + 1)
                if chunk == chunks - 1:
                    send_last_row(step + 1)

        for chunk in order:
            receive_planes(step, chunk)
            add_planes(step, chunk)
            if chunk == 0:

                @pl.when(at_axis)
                def _():
                    block_sums(step)

            else:
                finish(chunk)

        @pl.when(at_axis)
        def _():
            block_means(step)

        finish(0)

    for step in range(STEPS):
        for chunk in range(chunks):

            @pl.when(has_low)
            def _():
                to_low(step, chunk).wait_send()

            @pl.when(has_high)
            def _():
                to_high(step, chunk).wait_send()

            to_right(step, chunk).wait_send()
            if sectors > 2:
                to_left(step, chunk).wait_send()

        @pl.when(has_inner)
        def _():
            to_inner(step).wait_send()

        @pl.when(has_outer)
        def _():
            to_outer(step).wait_send()

        @pl.when(at_axis)
        def _():
            to_opposite(step).wait_send()
            for shift in range(1, sectors):
                to_sector(step, shift).wait_send()


def local(sizes, flow_state, cycle_widths):
    channels, planes, rows, columns = flow_state.shape
    rings = cycle_widths.shape[0]
    sectors = sizes[1]
    middle = rings + ((rows - rings) // 2 + 7) // 8 * 8
    bounds = (0, rings, middle, rows)
    chunks = len(bounds) - 1
    blocks = channels * planes
    f32 = jnp.float32
    dma = pltpu.SemaphoreType.DMA
    return pl.pallas_call(
        functools.partial(kernel, sizes, bounds),
        out_shape=jax.ShapeDtypeStruct(flow_state.shape, f32),
        in_specs=[
            pl.BlockSpec(memory_space=pl.ANY),
            pl.BlockSpec(memory_space=pltpu.SMEM),
        ],
        out_specs=pl.BlockSpec(memory_space=pltpu.VMEM),
        scratch_shapes=[
            pltpu.VMEM((STEPS, channels, planes, rows + 2 * PAD, columns), f32),
            pltpu.VMEM((channels, planes, rows, columns), f32),
            pltpu.VMEM((planes, rows, columns), f32),
            pltpu.VMEM((STEPS, channels, rows, columns), f32),
            pltpu.VMEM((STEPS, channels, rows, columns), f32),
            pltpu.VMEM((STEPS, rows, columns), f32),
            pltpu.VMEM((STEPS, rows, columns), f32),
            pltpu.VMEM((STEPS, rows, columns), f32),
            pltpu.VMEM((STEPS, 2, blocks, columns), f32),
            pltpu.VMEM((STEPS, 2, blocks, columns), f32),
            pltpu.VMEM((STEPS, rings, columns), f32),
            pltpu.VMEM((STEPS, sectors - 1, rings, columns), f32),
            dma,
            dma((STEPS, chunks)),
            dma((STEPS, chunks)),
            dma((STEPS, chunks)),
            dma((STEPS, chunks)),
            dma((STEPS, chunks)),
            dma((STEPS, chunks)),
            dma((STEPS, chunks)),
            dma((STEPS, chunks)),
            dma((STEPS, 2)),
            dma((STEPS, 2)),
            dma((STEPS,)),
            dma((STEPS,)),
            dma((STEPS, sectors - 1)),
            dma((STEPS, sectors - 1)),
        ],
        compiler_params=pltpu.CompilerParams(
            collective_id=0, has_side_effects=True, vmem_limit_bytes=32 * 1024 * 1024
        ),
    )(flow_state, cycle_widths)


def solution(mesh):
    sizes = (mesh.shape["ax"], mesh.shape["az"], mesh.shape["rad"])
    return jax.shard_map(
        functools.partial(local, sizes),
        mesh=mesh,
        in_specs=(P(None, ("groups", "ax"), "rad", "az"), P()),
        out_specs=P(None, ("groups", "ax"), "rad", "az"),
        check_vma=False,
    )
```

```python
import functools
import math

import jax
import jax.numpy as jnp
from jax import lax
from jax.experimental import pallas as pl
from jax.experimental.pallas import tpu as pltpu
from jax.sharding import PartitionSpec as P

STEPS = 2
DT = 0.2
KAPPA = 0.05
VISC = 0.1
RHO_RATIO = 20.0
PAD = 8
MESH = pl.DeviceIdType.MESH


def kernel(
    sizes,
    bounds,
    flow_ref,
    width_ref,
    out_ref,
    result,
    state,
    increment,
    spread,
    low_plane,
    high_plane,
    edge_out,
    edge_left,
    edge_right,
    row_out,
    row_in,
    circle,
    circle_increment,
    circle_spread,
    circle_low,
    circle_high,
    rim_in,
    basis,
    width_smem,
    load_sem,
    width_sem,
    circle_sem,
    out_sem,
    low_send,
    low_recv,
    high_send,
    high_recv,
    left_send,
    left_recv,
    right_send,
    right_recv,
    row_send,
    row_recv,
    gather_send,
    gather_recv,
    corner_low_send,
    corner_low_recv,
    corner_high_send,
    corner_high_recv,
    rim_send,
    rim_recv,
):
    axials, sectors, rads = sizes
    channels, planes, rows, columns = flow_ref.shape
    blocks = channels * planes
    rings = width_ref.shape[0]
    around = sectors * columns
    chunks = len(bounds) - 1
    ax = lax.axis_index("ax")
    az = lax.axis_index("az")
    rad = lax.axis_index("rad")
    angle_step = 2.0 * math.pi / (sectors * columns)
    half_arc = DT / (2.0 * angle_step)
    has_low = ax > 0
    has_high = ax < axials - 1
    has_inner = rad > 0
    has_outer = rad < rads - 1
    at_axis = rad == 0
    left = (az + sectors - 1) % sectors
    right = (az + 1) % sectors

    load = pltpu.make_async_copy(
        flow_ref, state.at[0, :, :, pl.ds(PAD, rows)], load_sem
    )
    load.start()
    load_width = pltpu.make_async_copy(width_ref, width_smem, width_sem)
    load_width.start()
    load_circle = pltpu.make_async_copy(
        flow_ref.at[:, :, pl.ds(0, rings + 8)],
        circle.at[0, :, :, pl.ds(PAD, rings + 8), pl.ds(0, columns)],
        circle_sem,
    )
    load_circle.start()

    barrier = pltpu.get_barrier_semaphore()

    def greet(axis, place):
        pl.semaphore_signal(barrier, inc=1, device_id={axis: place}, device_id_type=MESH)

    def greet_corner(place, shift):
        pl.semaphore_signal(
            barrier,
            inc=1,
            device_id={"ax": place, "az": (az + shift) % sectors},
            device_id_type=MESH,
        )

    @pl.when(has_low)
    def _():
        greet("ax", ax - 1)

    @pl.when(has_high)
    def _():
        greet("ax", ax + 1)

    @pl.when(has_inner)
    def _():
        greet("rad", rad - 1)

    @pl.when(has_outer)
    def _():
        greet("rad", rad + 1)

    for shift in range(1, sectors):
        greet("az", (az + shift) % sectors)

    @pl.when(jnp.logical_and(at_axis, has_low))
    def _():
        for shift in range(1, sectors):
            greet_corner(ax - 1, shift)

    @pl.when(jnp.logical_and(at_axis, has_high))
    def _():
        for shift in range(1, sectors):
            greet_corner(ax + 1, shift)

    def one(flag):
        return jnp.where(flag, 1, 0)

    pl.semaphore_wait(
        barrier,
        one(has_low)
        + one(has_high)
        + one(has_inner)
        + one(has_outer)
        + sectors
        - 1
        + one(at_axis) * (one(has_low) + one(has_high)) * (sectors - 1),
    )

    def remote(src, dst, send, recv, axis, place):
        return pltpu.make_async_remote_copy(
            src_ref=src,
            dst_ref=dst,
            send_sem=send,
            recv_sem=recv,
            device_id={axis: place},
            device_id_type=MESH,
        )

    def span(chunk):
        return pl.ds(bounds[chunk], bounds[chunk + 1] - bounds[chunk])

    def own(chunk):
        return pl.ds(PAD + bounds[chunk], bounds[chunk + 1] - bounds[chunk])

    def source(step, plane, chunk):
        if step == 0:
            return flow_ref.at[:, plane, span(chunk)]
        return state.at[step, :, plane, own(chunk)]

    def to_low(step, chunk):
        return remote(
            source(step, 0, chunk),
            high_plane.at[step, :, span(chunk)],
            low_send.at[step, chunk],
            low_recv.at[step, chunk],
            "ax",
            ax - 1,
        )

    def to_high(step, chunk):
        return remote(
            source(step, planes - 1, chunk),
            low_plane.at[step, :, span(chunk)],
            high_send.at[step, chunk],
            high_recv.at[step, chunk],
            "ax",
            ax + 1,
        )

    def to_right(step, chunk):
        return remote(
            edge_out.at[step, span(chunk)],
            edge_left.at[step, span(chunk)],
            right_send.at[step, chunk],
            right_recv.at[step, chunk],
            "az",
            right,
        )

    def to_left(step, chunk):
        return remote(
            edge_out.at[step, span(chunk)],
            edge_right.at[step, span(chunk)],
            left_send.at[step, chunk],
            left_recv.at[step, chunk],
            "az",
            left,
        )

    def to_inner(step):
        return remote(
            row_out.at[step, 0],
            row_in.at[step, 1],
            row_send.at[step, 0],
            row_recv.at[step, 0],
            "rad",
            rad - 1,
        )

    def to_outer(step):
        return remote(
            row_out.at[step, 1],
            row_in.at[step, 0],
            row_send.at[step, 1],
            row_recv.at[step, 1],
            "rad",
            rad + 1,
        )

    def circle_source(step, plane):
        if step == 0:
            return flow_ref.at[:, plane, pl.ds(0, rings)]
        return circle.at[step, :, plane, pl.ds(PAD, rings)]

    def circle_target(ref, step):
        if step == 0:
            return ref.at[step, :, :, pl.ds(0, columns)]
        return ref.at[step]

    def circle_to_low(step):
        return remote(
            circle_source(step, 0),
            circle_target(circle_high, step),
            low_send.at[step, 0],
            low_recv.at[step, 0],
            "ax",
            ax - 1,
        )

    def circle_to_high(step):
        return remote(
            circle_source(step, planes - 1),
            circle_target(circle_low, step),
            high_send.at[step, 0],
            high_recv.at[step, 0],
            "ax",
            ax + 1,
        )

    def corner_to_low(shift):
        return pltpu.make_async_remote_copy(
            src_ref=flow_ref.at[:, 0, pl.ds(0, rings)],
            dst_ref=circle_high.at[0, :, :, pl.ds((sectors - shift) * columns, columns)],
            send_sem=corner_low_send.at[shift - 1],
            recv_sem=corner_low_recv.at[shift - 1],
            device_id={"ax": ax - 1, "az": (az + shift) % sectors},
            device_id_type=MESH,
        )

    def corner_to_high(shift):
        return pltpu.make_async_remote_copy(
            src_ref=flow_ref.at[:, planes - 1, pl.ds(0, rings)],
            dst_ref=circle_low.at[0, :, :, pl.ds((sectors - shift) * columns, columns)],
            send_sem=corner_high_send.at[shift - 1],
            recv_sem=corner_high_recv.at[shift - 1],
            device_id={"ax": ax + 1, "az": (az + shift) % sectors},
            device_id_type=MESH,
        )

    def gather(shift):
        return remote(
            flow_ref.at[:, :, pl.ds(0, rings + 8)],
            circle.at[
                0, :, :, pl.ds(PAD, rings + 8), pl.ds((sectors - shift) * columns, columns)
            ],
            gather_send.at[shift - 1],
            gather_recv.at[shift - 1],
            "az",
            (az + shift) % sectors,
        )

    def to_rim(step, shift):
        return remote(
            row_out.at[step, 0],
            rim_in.at[step, sectors - shift - 1],
            rim_send.at[step, shift - 1],
            rim_recv.at[step, shift - 1],
            "az",
            (az + shift) % sectors,
        )

    def send_circle(step):
        @pl.when(has_low)
        def _():
            circle_to_low(step).start()
            if step == 0:
                for shift in range(1, sectors):
                    corner_to_low(shift).start()

        @pl.when(has_high)
        def _():
            circle_to_high(step).start()
            if step == 0:
                for shift in range(1, sectors):
                    corner_to_high(shift).start()

    def receive_circle(step):
        @pl.when(has_low)
        def _():
            circle_to_high(step).wait_recv()
            if step == 0:
                for shift in range(1, sectors):
                    corner_to_high(shift).wait_recv()

        @pl.when(has_high)
        def _():
            circle_to_low(step).wait_recv()
            if step == 0:
                for shift in range(1, sectors):
                    corner_to_low(shift).wait_recv()

    def send_rim(step):
        for block in range(blocks):
            row = state[step, block // planes, block % planes, pl.ds(PAD + rings, 1)]
            row_out[step, 0, pl.ds(block, 1)] = row
            circle[
                step, block // planes, block % planes, pl.ds(PAD + rings, 1), pl.ds(0, columns)
            ] = row
        for shift in range(1, sectors):
            to_rim(step, shift).start()

    def receive_rim(step):
        for shift in range(1, sectors):
            to_rim(step, shift).wait_recv()
            place = sectors - shift
            for block in range(blocks):
                circle[
                    step,
                    block // planes,
                    block % planes,
                    pl.ds(PAD + rings, 1),
                    pl.ds(place * columns, columns),
                ] = rim_in[step, place - 1, pl.ds(block, 1)]

    def send_planes(step, chunk):
        @pl.when(has_low)
        def _():
            to_low(step, chunk).start()

        @pl.when(has_high)
        def _():
            to_high(step, chunk).start()

    def send_edges(step, chunk):
        count = bounds[chunk + 1] - bounds[chunk]
        lane = lax.broadcasted_iota(jnp.int32, (count, columns), 1)
        packed = jnp.zeros((count, columns), jnp.float32)
        for block in range(blocks):
            values = state[step, block // planes, block % planes, own(chunk)]
            packed = jnp.where(
                lane // 2 == block, pltpu.roll(values, 2 * block + 1, 1), packed
            )
        edge_out[step, span(chunk)] = packed
        to_right(step, chunk).start()
        if sectors > 2:
            to_left(step, chunk).start()

    def send_first_row(step):
        for block in range(blocks):
            row_out[step, 0, pl.ds(block, 1)] = state[
                step, block // planes, block % planes, pl.ds(PAD, 1)
            ]

        to_inner(step).start()

    def send_last_row(step):
        for block in range(blocks):
            row_out[step, 1, pl.ds(block, 1)] = state[
                step, block // planes, block % planes, pl.ds(PAD + rows - 1, 1)
            ]

        @pl.when(has_outer)
        def _():
            to_outer(step).start()

    def receive_rows(step):
        @pl.when(has_inner)
        def _():
            to_outer(step).wait_recv()
            for block in range(blocks):
                state[step, block // planes, block % planes, pl.ds(PAD - 1, 1)] = row_in[
                    step, 0, pl.ds(block, 1)
                ]

        @pl.when(has_outer)
        def _():
            to_inner(step).wait_recv()
            for block in range(blocks):
                state[step, block // planes, block % planes, pl.ds(PAD + rows, 1)] = row_in[
                    step, 1, pl.ds(block, 1)
                ]

        @pl.when(jnp.logical_not(has_outer))
        def _():
            for block in range(blocks):
                state[step, block // planes, block % planes, pl.ds(PAD + rows, 1)] = jnp.zeros(
                    (1, columns), jnp.float32
                )

    def terms(start, shape):
        row = lax.broadcasted_iota(jnp.int32, shape, 0)
        radius = (rad * rows + start + row).astype(jnp.float32) + 0.5
        reciprocal = 1.0 / radius
        return (
            reciprocal,
            half_arc * reciprocal,
            1.0 + 0.5 * reciprocal,
            1.0 - 0.5 * reciprocal,
            (0.5 * DT) * (1.0 + reciprocal),
            (0.5 * DT) * (1.0 - reciprocal),
        )

    def plane_rates(weights, center, outer, inner, ahead, behind, upper, lower):
        reciprocal, arc, outer_weight, inner_weight, outer_flux, inner_flux = weights
        level, axial, radial, swirl = center
        density = 1.0 + (RHO_RATIO - 1.0) * jnp.clip(level, 0.0, 1.0)
        thin = (DT * VISC) / density
        laplace = [
            outer_weight * outer[c] + inner_weight * inner[c] - 4.0 * center[c]
            for c in range(channels)
        ]
        for other in (upper, lower):
            if other is not None:
                laplace = [laplace[c] + other[c] for c in range(channels)]
        rate = (
            (DT * KAPPA) * laplace[0]
            - outer_flux * outer[2] * outer[0]
            + inner_flux * inner[2] * inner[0]
            - arc * (ahead[3] * ahead[0] - behind[3] * behind[0])
        )
        if upper is not None:
            rate = rate - (0.5 * DT) * upper[1] * upper[0]
        if lower is not None:
            rate = rate + (0.5 * DT) * lower[1] * lower[0]
        found = [rate]
        drift = (0.5 * DT) * axial
        push = (0.5 * DT) * radial
        turn = arc * swirl
        for c in range(1, channels):
            rate = (
                thin * laplace[c]
                - push * (outer[c] - inner[c])
                - turn * (ahead[c] - behind[c])
            )
            if upper is not None:
                rate = rate - drift * upper[c]
            if lower is not None:
                rate = rate + drift * lower[c]
            if c == 2:
                rate = rate + (DT * reciprocal) * swirl * swirl
            if c == 3:
                rate = rate - (DT * reciprocal) * swirl * radial
            found.append(rate)
        return thin, found

    def in_plane(step, chunk):
        to_right(step, chunk).wait_recv()
        if sectors > 2:
            to_left(step, chunk).wait_recv()
        for start in range(bounds[chunk], bounds[chunk + 1], 8):
            shape = (8, columns)
            lane = lax.broadcasted_iota(jnp.int32, shape, 1)
            weights = terms(start, shape)
            edges = edge_left[step, pl.ds(start, 8)]
            if sectors > 2:
                edges = jnp.where(lane % 2 == 0, edges, edge_right[step, pl.ds(start, 8)])

            def cell(channel, plane, offset=0):
                return state[step, channel, plane, pl.ds(PAD + start + offset, 8)]

            def cells(plane, offset=0):
                return [cell(c, plane, offset) for c in range(channels)]

            for plane in range(planes):
                center = cells(plane)
                ahead, behind = [], []
                for c in range(channels):
                    block = c * planes + plane
                    rim = pltpu.roll(edges, (columns - 2 * block - 1) % columns, 1)
                    ahead.append(
                        pltpu.roll(jnp.where(lane == 0, rim, center[c]), columns - 1, 1)
                    )
                    behind.append(
                        pltpu.roll(jnp.where(lane == columns - 1, rim, center[c]), 1, 1)
                    )
                thin, rate = plane_rates(
                    weights,
                    center,
                    cells(plane, 1),
                    cells(plane, -1),
                    ahead,
                    behind,
                    cells(plane + 1) if plane < planes - 1 else None,
                    cells(plane - 1) if plane > 0 else None,
                )
                spread[plane, pl.ds(start, 8)] = thin
                for c in range(channels):
                    increment[c, plane, pl.ds(start, 8)] = rate[c]

    def in_circle(step):
        if step == 0:
            load_circle.wait()
            for shift in range(1, sectors):
                gather(shift).wait_recv()
        else:
            receive_rim(step)
        for c in range(channels):
            sign = 1.0 if c < 2 else -1.0
            for plane in range(planes):
                first = circle[step, c, plane, pl.ds(PAD, 8)]
                circle[step, c, plane, pl.ds(PAD - 1, 1)] = (
                    sign * pltpu.roll(first, around // 2, 1)[:1]
                )
        for start in range(0, rings, 8):
            weights = terms(start, (8, around))

            def cells(plane, offset=0):
                return [
                    circle[step, c, plane, pl.ds(PAD + start + offset, 8)]
                    for c in range(channels)
                ]

            for plane in range(planes):
                center = cells(plane)
                thin, rate = plane_rates(
                    weights,
                    center,
                    cells(plane, 1),
                    cells(plane, -1),
                    [pltpu.roll(x, around - 1, 1) for x in center],
                    [pltpu.roll(x, 1, 1) for x in center],
                    cells(plane + 1) if plane < planes - 1 else None,
                    cells(plane - 1) if plane > 0 else None,
                )
                circle_spread[plane, pl.ds(start, 8)] = thin
                for c in range(channels):
                    circle_increment[c, plane, pl.ds(start, 8)] = rate[c]

    def receive_planes(step, chunk):
        @pl.when(has_low)
        def _():
            to_high(step, chunk).wait_recv()

        @pl.when(has_high)
        def _():
            to_low(step, chunk).wait_recv()

    def add_planes(step, chunk):
        for plane, halo, sign in ((0, low_plane, 1.0), (planes - 1, high_plane, -1.0)):
            here = span(chunk)
            drift = (sign * 0.5 * DT) * state[step, 1, plane, own(chunk)]
            weight = drift + spread[plane, here]
            level = halo[step, 0, here]
            increment[0, plane, here] += level * (
                DT * KAPPA + (sign * 0.5 * DT) * halo[step, 1, here]
            )
            for c in range(1, channels):
                increment[c, plane, here] += weight * halo[step, c, here]

    def store(step, chunk):
        for c in range(channels):
            for plane in range(planes):
                value = state[step, c, plane, own(chunk)] + increment[c, plane, span(chunk)]
                if step == STEPS - 1:
                    result[c, plane, span(chunk)] = value
                else:
                    state[step + 1, c, plane, own(chunk)] = value

    def add_circle(step):
        for plane, halo, sign in ((0, circle_low, 1.0), (planes - 1, circle_high, -1.0)):
            drift = (sign * 0.5 * DT) * circle[step, 1, plane, pl.ds(PAD, rings)]
            weight = drift + circle_spread[plane]
            circle_increment[0, plane] += halo[step, 0] * (
                DT * KAPPA + (sign * 0.5 * DT) * halo[step, 1]
            )
            for c in range(1, channels):
                circle_increment[c, plane] += weight * halo[step, c]

    level_count = columns.bit_length() - 1

    def make_basis():
        for level in range(level_count):
            width = 2 << level
            shape = (2 * columns, columns)
            row = lax.broadcasted_iota(jnp.int32, shape, 0) % columns
            lane = lax.broadcasted_iota(jnp.int32, shape, 1)
            same = jnp.where(row // width == lane // width, 1.0 / width, 0.0)
            basis[:, pl.ds(level * columns, columns)] = same.astype(jnp.bfloat16)

    def block_means(step):
        shape = (8, columns)
        row = lax.broadcasted_iota(jnp.int32, shape, 0)
        for start in range(0, rings, 8):
            width = jnp.zeros(shape, jnp.int32)
            for ring in range(8):
                width = jnp.where(row == ring, width_smem[start + ring], width)
            values = jnp.concatenate(
                [
                    circle_increment[
                        block // planes,
                        block % planes,
                        pl.ds(start, 8),
                        pl.ds(sector * columns, columns),
                    ]
                    for block in range(blocks)
                    for sector in range(sectors)
                ],
                axis=0,
            )
            coarse = values.astype(jnp.bfloat16)
            fine = (values - coarse.astype(jnp.float32)).astype(jnp.bfloat16)
            means = jnp.dot(
                jnp.concatenate([coarse, fine], axis=1),
                basis[...],
                preferred_element_type=jnp.float32,
            )
            for block in range(blocks):
                picked, whole = [], []
                for sector in range(sectors):
                    first = (block * sectors + sector) * 8
                    mean = None
                    for level in range(level_count):
                        part = means[
                            first : first + 8, level * columns : (level + 1) * columns
                        ]
                        if mean is None:
                            mean = part
                        else:
                            mean = jnp.where(width == 2 << level, part, mean)
                    whole.append(part)
                    picked.append(mean)
                size = 2
                while size <= sectors:
                    for sector in range(sectors):
                        total = jnp.zeros(shape, jnp.float32)
                        for other in range(sectors):
                            if size == sectors:
                                total = total + whole[other]
                            else:
                                same = (az + sector) % sectors // size == (
                                    az + other
                                ) % sectors // size
                                total = total + jnp.where(same, 1.0, 0.0) * whole[other]
                        picked[sector] = jnp.where(
                            width == size * columns, total * (1.0 / size), picked[sector]
                        )
                    size *= 2
                c, plane = block // planes, block % planes
                here = pl.ds(PAD + start, 8)
                for sector in range(sectors):
                    lanes = pl.ds(sector * columns, columns)
                    if step == STEPS - 1 and sector > 0:
                        continue
                    value = circle[step, c, plane, here, lanes] + picked[sector]
                    if step == STEPS - 1:
                        result[c, plane, pl.ds(start, 8)] = value
                    else:
                        circle[step + 1, c, plane, here, lanes] = value
                        if sector == 0:
                            state[step + 1, c, plane, here] = value

    def unload(chunk):
        return pltpu.make_async_copy(
            result.at[:, :, span(chunk)], out_ref.at[:, :, span(chunk)], out_sem.at[chunk]
        )

    off_axis = jnp.logical_not(at_axis)

    @pl.when(at_axis)
    def _():
        send_circle(0)
        for shift in range(1, sectors):
            gather(shift).start()

    @pl.when(off_axis)
    def _():
        send_planes(0, 0)

    for chunk in range(1, chunks):
        send_planes(0, chunk)

    @pl.when(jnp.logical_not(has_low))
    def _():
        low_plane[...] = jnp.zeros(low_plane.shape, jnp.float32)
        circle_low[...] = jnp.zeros(circle_low.shape, jnp.float32)

    @pl.when(jnp.logical_not(has_high))
    def _():
        high_plane[...] = jnp.zeros(high_plane.shape, jnp.float32)
        circle_high[...] = jnp.zeros(circle_high.shape, jnp.float32)

    load.wait()
    send_last_row(0)

    @pl.when(off_axis)
    def _():
        send_first_row(0)
        send_edges(0, 0)

    for chunk in range(1, chunks):
        send_edges(0, chunk)

    @pl.when(at_axis)
    def _():
        make_basis()

    load_width.wait()
    for step in range(STEPS):
        last = step == STEPS - 1
        receive_rows(step)

        @pl.when(at_axis)
        def _():
            in_circle(step)
            receive_circle(step)
            add_circle(step)
            block_means(step)
            if last:
                unload(0).start()
            else:
                send_circle(step + 1)

        @pl.when(off_axis)
        def _():
            in_plane(step, 0)

        for chunk in range(1, chunks):
            in_plane(step, chunk)

        @pl.when(off_axis)
        def _():
            receive_planes(step, 0)
            add_planes(step, 0)
            store(step, 0)
            if last:
                unload(0).start()
            else:
                send_planes(step + 1, 0)
                send_edges(step + 1, 0)
                send_first_row(step + 1)

        for chunk in range(1, chunks):
            receive_planes(step, chunk)
            add_planes(step, chunk)
            store(step, chunk)
            if last:
                unload(chunk).start()
            else:
                send_planes(step + 1, chunk)
                send_edges(step + 1, chunk)
                if chunk == 1:

                    @pl.when(at_axis)
                    def _():
                        send_rim(step + 1)

                if chunk == chunks - 1:
                    send_last_row(step + 1)

    @pl.when(off_axis)
    def _():
        load_circle.wait()

    for step in range(STEPS):
        for chunk in range(chunks):

            def sent():
                @pl.when(has_low)
                def _():
                    to_low(step, chunk).wait_send()

                @pl.when(has_high)
                def _():
                    to_high(step, chunk).wait_send()

                to_right(step, chunk).wait_send()
                if sectors > 2:
                    to_left(step, chunk).wait_send()

            if chunk == 0:
                pl.when(off_axis)(sent)
            else:
                sent()

        @pl.when(has_inner)
        def _():
            to_inner(step).wait_send()

        @pl.when(has_outer)
        def _():
            to_outer(step).wait_send()

        @pl.when(at_axis)
        def _():
            @pl.when(has_low)
            def _():
                circle_to_low(step).wait_send()
                if step == 0:
                    for shift in range(1, sectors):
                        corner_to_low(shift).wait_send()

            @pl.when(has_high)
            def _():
                circle_to_high(step).wait_send()
                if step == 0:
                    for shift in range(1, sectors):
                        corner_to_high(shift).wait_send()

            for shift in range(1, sectors):
                if step == 0:
                    gather(shift).wait_send()
                else:
                    to_rim(step, shift).wait_send()

    for chunk in range(chunks):
        unload(chunk).wait()


def local(sizes, flow_state, cycle_widths):
    channels, planes, rows, columns = flow_state.shape
    rings = cycle_widths.shape[0]
    sectors = sizes[1]
    middle = rings + ((rows - rings) // 2 + 7) // 8 * 8
    bounds = (0, rings, middle, rows)
    chunks = len(bounds) - 1
    blocks = channels * planes
    around = sectors * columns
    f32 = jnp.float32
    dma = pltpu.SemaphoreType.DMA
    return pl.pallas_call(
        functools.partial(kernel, sizes, bounds),
        out_shape=jax.ShapeDtypeStruct(flow_state.shape, f32),
        in_specs=[
            pl.BlockSpec(memory_space=pl.ANY),
            pl.BlockSpec(memory_space=pl.ANY),
        ],
        out_specs=pl.BlockSpec(memory_space=pl.ANY),
        scratch_shapes=[
            pltpu.VMEM((channels, planes, rows, columns), f32),
            pltpu.VMEM((STEPS, channels, planes, rows + 2 * PAD, columns), f32),
            pltpu.VMEM((channels, planes, rows, columns), f32),
            pltpu.VMEM((planes, rows, columns), f32),
            pltpu.VMEM((STEPS, channels, rows, columns), f32),
            pltpu.VMEM((STEPS, channels, rows, columns), f32),
            pltpu.VMEM((STEPS, rows, columns), f32),
            pltpu.VMEM((STEPS, rows, columns), f32),
            pltpu.VMEM((STEPS, rows, columns), f32),
            pltpu.VMEM((STEPS, 2, blocks, columns), f32),
            pltpu.VMEM((STEPS, 2, blocks, columns), f32),
            pltpu.VMEM((STEPS, channels, planes, rings + 2 * PAD, around), f32),
            pltpu.VMEM((channels, planes, rings, around), f32),
            pltpu.VMEM((planes, rings, around), f32),
            pltpu.VMEM((STEPS, channels, rings, around), f32),
            pltpu.VMEM((STEPS, channels, rings, around), f32),
            pltpu.VMEM((STEPS, sectors - 1, blocks, columns), f32),
            pltpu.VMEM((2 * columns, (columns.bit_length() - 1) * columns), jnp.bfloat16),
            pltpu.SMEM((rings,), jnp.int32),
            dma,
            dma,
            dma,
            dma((chunks,)),
            dma((STEPS, chunks)),
            dma((STEPS, chunks)),
            dma((STEPS, chunks)),
            dma((STEPS, chunks)),
            dma((STEPS, chunks)),
            dma((STEPS, chunks)),
            dma((STEPS, chunks)),
            dma((STEPS, chunks)),
            dma((STEPS, 2)),
            dma((STEPS, 2)),
            dma((sectors - 1,)),
            dma((sectors - 1,)),
            dma((sectors - 1,)),
            dma((sectors - 1,)),
            dma((sectors - 1,)),
            dma((sectors - 1,)),
            dma((STEPS, sectors - 1)),
            dma((STEPS, sectors - 1)),
        ],
        compiler_params=pltpu.CompilerParams(
            collective_id=0, has_side_effects=True, vmem_limit_bytes=64 * 1024 * 1024
        ),
    )(flow_state, cycle_widths)


def solution(mesh):
    sizes = (mesh.shape["ax"], mesh.shape["az"], mesh.shape["rad"])
    return jax.shard_map(
        functools.partial(local, sizes),
        mesh=mesh,
        in_specs=(P(None, ("groups", "ax"), "rad", "az"), P()),
        out_specs=P(None, ("groups", "ax"), "rad", "az"),
        check_vma=False,
    )
```

```python
import functools
import math

import jax
import jax.numpy as jnp
from jax import lax
from jax.experimental import pallas as pl
from jax.experimental.pallas import tpu as pltpu
from jax.sharding import PartitionSpec as P

STEPS = 2
DT = 0.2
KAPPA = 0.05
VISC = 0.1
RHO_RATIO = 20.0
PAD = 8
MESH = pl.DeviceIdType.MESH


def kernel(
    sizes,
    bounds,
    flow_ref,
    width_ref,
    out_ref,
    state,
    increment,
    spread,
    low_plane,
    high_plane,
    edge_out,
    edge_left,
    edge_right,
    row_out,
    row_in,
    circle,
    circle_increment,
    circle_spread,
    circle_low,
    circle_high,
    rim_in,
    basis,
    width_smem,
    load_sem,
    width_sem,
    circle_sem,
    low_send,
    low_recv,
    high_send,
    high_recv,
    left_send,
    left_recv,
    right_send,
    right_recv,
    row_send,
    row_recv,
    gather_send,
    gather_recv,
    corner_low_send,
    corner_low_recv,
    corner_high_send,
    corner_high_recv,
    rim_send,
    rim_recv,
):
    axials, sectors, rads = sizes
    channels, planes, rows, columns = flow_ref.shape
    blocks = channels * planes
    rings = width_ref.shape[0]
    around = sectors * columns
    chunks = len(bounds) - 1
    ax = lax.axis_index("ax")
    az = lax.axis_index("az")
    rad = lax.axis_index("rad")
    angle_step = 2.0 * math.pi / (sectors * columns)
    half_arc = DT / (2.0 * angle_step)
    has_low = ax > 0
    has_high = ax < axials - 1
    has_inner = rad > 0
    has_outer = rad < rads - 1
    at_axis = rad == 0
    left = (az + sectors - 1) % sectors
    right = (az + 1) % sectors

    load = pltpu.make_async_copy(
        flow_ref, state.at[0, :, :, pl.ds(PAD, rows)], load_sem
    )
    load.start()
    load_width = pltpu.make_async_copy(width_ref, width_smem, width_sem)
    load_width.start()
    load_circle = pltpu.make_async_copy(
        flow_ref.at[:, :, pl.ds(0, rings + 8)],
        circle.at[0, :, :, pl.ds(PAD, rings + 8), pl.ds(0, columns)],
        circle_sem,
    )
    load_circle.start()

    barrier = pltpu.get_barrier_semaphore()

    def greet(axis, place):
        pl.semaphore_signal(barrier, inc=1, device_id={axis: place}, device_id_type=MESH)

    def greet_corner(place, shift):
        pl.semaphore_signal(
            barrier,
            inc=1,
            device_id={"ax": place, "az": (az + shift) % sectors},
            device_id_type=MESH,
        )

    @pl.when(has_low)
    def _():
        greet("ax", ax - 1)

    @pl.when(has_high)
    def _():
        greet("ax", ax + 1)

    @pl.when(has_inner)
    def _():
        greet("rad", rad - 1)

    @pl.when(has_outer)
    def _():
        greet("rad", rad + 1)

    for shift in range(1, sectors):
        greet("az", (az + shift) % sectors)

    @pl.when(jnp.logical_and(at_axis, has_low))
    def _():
        for shift in range(1, sectors):
            greet_corner(ax - 1, shift)

    @pl.when(jnp.logical_and(at_axis, has_high))
    def _():
        for shift in range(1, sectors):
            greet_corner(ax + 1, shift)

    def one(flag):
        return jnp.where(flag, 1, 0)

    pl.semaphore_wait(
        barrier,
        one(has_low)
        + one(has_high)
        + one(has_inner)
        + one(has_outer)
        + sectors
        - 1
        + one(at_axis) * (one(has_low) + one(has_high)) * (sectors - 1),
    )

    def remote(src, dst, send, recv, axis, place):
        return pltpu.make_async_remote_copy(
            src_ref=src,
            dst_ref=dst,
            send_sem=send,
            recv_sem=recv,
            device_id={axis: place},
            device_id_type=MESH,
        )

    def span(chunk):
        return pl.ds(bounds[chunk], bounds[chunk + 1] - bounds[chunk])

    def own(chunk):
        return pl.ds(PAD + bounds[chunk], bounds[chunk + 1] - bounds[chunk])

    def source(step, plane, chunk):
        if step == 0:
            return flow_ref.at[:, plane, span(chunk)]
        return state.at[step, :, plane, own(chunk)]

    def to_low(step, chunk):
        return remote(
            source(step, 0, chunk),
            high_plane.at[step, :, span(chunk)],
            low_send.at[step, chunk],
            low_recv.at[step, chunk],
            "ax",
            ax - 1,
        )

    def to_high(step, chunk):
        return remote(
            source(step, planes - 1, chunk),
            low_plane.at[step, :, span(chunk)],
            high_send.at[step, chunk],
            high_recv.at[step, chunk],
            "ax",
            ax + 1,
        )

    def to_right(step, chunk):
        return remote(
            edge_out.at[step, span(chunk)],
            edge_left.at[step, span(chunk)],
            right_send.at[step, chunk],
            right_recv.at[step, chunk],
            "az",
            right,
        )

    def to_left(step, chunk):
        return remote(
            edge_out.at[step, span(chunk)],
            edge_right.at[step, span(chunk)],
            left_send.at[step, chunk],
            left_recv.at[step, chunk],
            "az",
            left,
        )

    def to_inner(step):
        return remote(
            row_out.at[step, 0],
            row_in.at[step, 1],
            row_send.at[step, 0],
            row_recv.at[step, 0],
            "rad",
            rad - 1,
        )

    def to_outer(step):
        return remote(
            row_out.at[step, 1],
            row_in.at[step, 0],
            row_send.at[step, 1],
            row_recv.at[step, 1],
            "rad",
            rad + 1,
        )

    def circle_source(step, plane):
        if step == 0:
            return flow_ref.at[:, plane, pl.ds(0, rings)]
        return circle.at[step, :, plane, pl.ds(PAD, rings)]

    def circle_target(ref, step):
        if step == 0:
            return ref.at[step, :, :, pl.ds(0, columns)]
        return ref.at[step]

    def circle_to_low(step):
        return remote(
            circle_source(step, 0),
            circle_target(circle_high, step),
            low_send.at[step, 0],
            low_recv.at[step, 0],
            "ax",
            ax - 1,
        )

    def circle_to_high(step):
        return remote(
            circle_source(step, planes - 1),
            circle_target(circle_low, step),
            high_send.at[step, 0],
            high_recv.at[step, 0],
            "ax",
            ax + 1,
        )

    def corner_to_low(shift):
        return pltpu.make_async_remote_copy(
            src_ref=flow_ref.at[:, 0, pl.ds(0, rings)],
            dst_ref=circle_high.at[0, :, :, pl.ds((sectors - shift) * columns, columns)],
            send_sem=corner_low_send.at[shift - 1],
            recv_sem=corner_low_recv.at[shift - 1],
            device_id={"ax": ax - 1, "az": (az + shift) % sectors},
            device_id_type=MESH,
        )

    def corner_to_high(shift):
        return pltpu.make_async_remote_copy(
            src_ref=flow_ref.at[:, planes - 1, pl.ds(0, rings)],
            dst_ref=circle_low.at[0, :, :, pl.ds((sectors - shift) * columns, columns)],
            send_sem=corner_high_send.at[shift - 1],
            recv_sem=corner_high_recv.at[shift - 1],
            device_id={"ax": ax + 1, "az": (az + shift) % sectors},
            device_id_type=MESH,
        )

    def gather(shift):
        return remote(
            flow_ref.at[:, :, pl.ds(0, rings + 8)],
            circle.at[
                0, :, :, pl.ds(PAD, rings + 8), pl.ds((sectors - shift) * columns, columns)
            ],
            gather_send.at[shift - 1],
            gather_recv.at[shift - 1],
            "az",
            (az + shift) % sectors,
        )

    def to_rim(step, shift):
        return remote(
            row_out.at[step, 0],
            rim_in.at[step, sectors - shift - 1],
            rim_send.at[step, shift - 1],
            rim_recv.at[step, shift - 1],
            "az",
            (az + shift) % sectors,
        )

    def send_circle(step):
        @pl.when(has_low)
        def _():
            circle_to_low(step).start()
            if step == 0:
                for shift in range(1, sectors):
                    corner_to_low(shift).start()

        @pl.when(has_high)
        def _():
            circle_to_high(step).start()
            if step == 0:
                for shift in range(1, sectors):
                    corner_to_high(shift).start()

    def receive_circle(step):
        @pl.when(has_low)
        def _():
            circle_to_high(step).wait_recv()
            if step == 0:
                for shift in range(1, sectors):
                    corner_to_high(shift).wait_recv()

        @pl.when(has_high)
        def _():
            circle_to_low(step).wait_recv()
            if step == 0:
                for shift in range(1, sectors):
                    corner_to_low(shift).wait_recv()

    def send_rim(step):
        for block in range(blocks):
            row = state[step, block // planes, block % planes, pl.ds(PAD + rings, 1)]
            row_out[step, 0, pl.ds(block, 1)] = row
            circle[
                step, block // planes, block % planes, pl.ds(PAD + rings, 1), pl.ds(0, columns)
            ] = row
        for shift in range(1, sectors):
            to_rim(step, shift).start()

    def receive_rim(step):
        for shift in range(1, sectors):
            to_rim(step, shift).wait_recv()
            place = sectors - shift
            for block in range(blocks):
                circle[
                    step,
                    block // planes,
                    block % planes,
                    pl.ds(PAD + rings, 1),
                    pl.ds(place * columns, columns),
                ] = rim_in[step, place - 1, pl.ds(block, 1)]

    def send_planes(step, chunk):
        @pl.when(has_low)
        def _():
            to_low(step, chunk).start()

        @pl.when(has_high)
        def _():
            to_high(step, chunk).start()

    def send_edges(step, chunk):
        count = bounds[chunk + 1] - bounds[chunk]
        lane = lax.broadcasted_iota(jnp.int32, (count, columns), 1)
        packed = jnp.zeros((count, columns), jnp.float32)
        for block in range(blocks):
            values = state[step, block // planes, block % planes, own(chunk)]
            packed = jnp.where(
                lane // 2 == block, pltpu.roll(values, 2 * block + 1, 1), packed
            )
        edge_out[step, span(chunk)] = packed
        to_right(step, chunk).start()
        if sectors > 2:
            to_left(step, chunk).start()

    def send_first_row(step):
        for block in range(blocks):
            row_out[step, 0, pl.ds(block, 1)] = state[
                step, block // planes, block % planes, pl.ds(PAD, 1)
            ]

        to_inner(step).start()

    def send_last_row(step):
        for block in range(blocks):
            row_out[step, 1, pl.ds(block, 1)] = state[
                step, block // planes, block % planes, pl.ds(PAD + rows - 1, 1)
            ]

        @pl.when(has_outer)
        def _():
            to_outer(step).start()

    def receive_rows(step):
        @pl.when(has_inner)
        def _():
            to_outer(step).wait_recv()
            for block in range(blocks):
                state[step, block // planes, block % planes, pl.ds(PAD - 1, 1)] = row_in[
                    step, 0, pl.ds(block, 1)
                ]

        @pl.when(has_outer)
        def _():
            to_inner(step).wait_recv()
            for block in range(blocks):
                state[step, block // planes, block % planes, pl.ds(PAD + rows, 1)] = row_in[
                    step, 1, pl.ds(block, 1)
                ]

        @pl.when(jnp.logical_not(has_outer))
        def _():
            for block in range(blocks):
                state[step, block // planes, block % planes, pl.ds(PAD + rows, 1)] = jnp.zeros(
                    (1, columns), jnp.float32
                )

    def terms(start, shape):
        row = lax.broadcasted_iota(jnp.int32, shape, 0)
        radius = (rad * rows + start + row).astype(jnp.float32) + 0.5
        reciprocal = 1.0 / radius
        return (
            reciprocal,
            half_arc * reciprocal,
            1.0 + 0.5 * reciprocal,
            1.0 - 0.5 * reciprocal,
            (0.5 * DT) * (1.0 + reciprocal),
            (0.5 * DT) * (1.0 - reciprocal),
        )

    def plane_rates(weights, center, outer, inner, ahead, behind, upper, lower):
        reciprocal, arc, outer_weight, inner_weight, outer_flux, inner_flux = weights
        level, axial, radial, swirl = center
        density = 1.0 + (RHO_RATIO - 1.0) * jnp.clip(level, 0.0, 1.0)
        thin = (DT * VISC) / density
        laplace = [
            outer_weight * outer[c] + inner_weight * inner[c] - 4.0 * center[c]
            for c in range(channels)
        ]
        for other in (upper, lower):
            if other is not None:
                laplace = [laplace[c] + other[c] for c in range(channels)]
        rate = (
            (DT * KAPPA) * laplace[0]
            - outer_flux * outer[2] * outer[0]
            + inner_flux * inner[2] * inner[0]
            - arc * (ahead[3] * ahead[0] - behind[3] * behind[0])
        )
        if upper is not None:
            rate = rate - (0.5 * DT) * upper[1] * upper[0]
        if lower is not None:
            rate = rate + (0.5 * DT) * lower[1] * lower[0]
        found = [rate]
        drift = (0.5 * DT) * axial
        push = (0.5 * DT) * radial
        turn = arc * swirl
        for c in range(1, channels):
            rate = (
                thin * laplace[c]
                - push * (outer[c] - inner[c])
                - turn * (ahead[c] - behind[c])
            )
            if upper is not None:
                rate = rate - drift * upper[c]
            if lower is not None:
                rate = rate + drift * lower[c]
            if c == 2:
                rate = rate + (DT * reciprocal) * swirl * swirl
            if c == 3:
                rate = rate - (DT * reciprocal) * swirl * radial
            found.append(rate)
        return thin, found

    def in_plane(step, chunk):
        to_right(step, chunk).wait_recv()
        if sectors > 2:
            to_left(step, chunk).wait_recv()
        for start in range(bounds[chunk], bounds[chunk + 1], 8):
            shape = (8, columns)
            lane = lax.broadcasted_iota(jnp.int32, shape, 1)
            weights = terms(start, shape)
            edges = edge_left[step, pl.ds(start, 8)]
            if sectors > 2:
                edges = jnp.where(lane % 2 == 0, edges, edge_right[step, pl.ds(start, 8)])

            def cell(channel, plane, offset=0):
                return state[step, channel, plane, pl.ds(PAD + start + offset, 8)]

            def cells(plane, offset=0):
                return [cell(c, plane, offset) for c in range(channels)]

            for plane in range(planes):
                center = cells(plane)
                ahead, behind = [], []
                for c in range(channels):
                    block = c * planes + plane
                    rim = pltpu.roll(edges, (columns - 2 * block - 1) % columns, 1)
                    ahead.append(
                        pltpu.roll(jnp.where(lane == 0, rim, center[c]), columns - 1, 1)
                    )
                    behind.append(
                        pltpu.roll(jnp.where(lane == columns - 1, rim, center[c]), 1, 1)
                    )
                thin, rate = plane_rates(
                    weights,
                    center,
                    cells(plane, 1),
                    cells(plane, -1),
                    ahead,
                    behind,
                    cells(plane + 1) if plane < planes - 1 else None,
                    cells(plane - 1) if plane > 0 else None,
                )
                spread[plane, pl.ds(start, 8)] = thin
                for c in range(channels):
                    increment[c, plane, pl.ds(start, 8)] = rate[c]

    def in_circle(step):
        if step == 0:
            load_circle.wait()
            for shift in range(1, sectors):
                gather(shift).wait_recv()
        else:
            receive_rim(step)
        for c in range(channels):
            sign = 1.0 if c < 2 else -1.0
            for plane in range(planes):
                first = circle[step, c, plane, pl.ds(PAD, 8)]
                circle[step, c, plane, pl.ds(PAD - 1, 1)] = (
                    sign * pltpu.roll(first, around // 2, 1)[:1]
                )
        for start in range(0, rings, 8):
            weights = terms(start, (8, around))

            def cells(plane, offset=0):
                return [
                    circle[step, c, plane, pl.ds(PAD + start + offset, 8)]
                    for c in range(channels)
                ]

            for plane in range(planes):
                center = cells(plane)
                thin, rate = plane_rates(
                    weights,
                    center,
                    cells(plane, 1),
                    cells(plane, -1),
                    [pltpu.roll(x, around - 1, 1) for x in center],
                    [pltpu.roll(x, 1, 1) for x in center],
                    cells(plane + 1) if plane < planes - 1 else None,
                    cells(plane - 1) if plane > 0 else None,
                )
                circle_spread[plane, pl.ds(start, 8)] = thin
                for c in range(channels):
                    circle_increment[c, plane, pl.ds(start, 8)] = rate[c]

    def receive_planes(step, chunk):
        @pl.when(has_low)
        def _():
            to_high(step, chunk).wait_recv()

        @pl.when(has_high)
        def _():
            to_low(step, chunk).wait_recv()

    def add_planes(step, chunk):
        for plane, halo, sign in ((0, low_plane, 1.0), (planes - 1, high_plane, -1.0)):
            here = span(chunk)
            drift = (sign * 0.5 * DT) * state[step, 1, plane, own(chunk)]
            weight = drift + spread[plane, here]
            level = halo[step, 0, here]
            increment[0, plane, here] += level * (
                DT * KAPPA + (sign * 0.5 * DT) * halo[step, 1, here]
            )
            for c in range(1, channels):
                increment[c, plane, here] += weight * halo[step, c, here]

    def store(step, chunk):
        for c in range(channels):
            for plane in range(planes):
                value = state[step, c, plane, own(chunk)] + increment[c, plane, span(chunk)]
                if step == STEPS - 1:
                    out_ref[c, plane, span(chunk)] = value
                else:
                    state[step + 1, c, plane, own(chunk)] = value

    def add_circle(step):
        for plane, halo, sign in ((0, circle_low, 1.0), (planes - 1, circle_high, -1.0)):
            drift = (sign * 0.5 * DT) * circle[step, 1, plane, pl.ds(PAD, rings)]
            weight = drift + circle_spread[plane]
            circle_increment[0, plane] += halo[step, 0] * (
                DT * KAPPA + (sign * 0.5 * DT) * halo[step, 1]
            )
            for c in range(1, channels):
                circle_increment[c, plane] += weight * halo[step, c]

    level_count = columns.bit_length() - 1

    def make_basis():
        for level in range(level_count):
            width = 2 << level
            shape = (2 * columns, columns)
            row = lax.broadcasted_iota(jnp.int32, shape, 0) % columns
            lane = lax.broadcasted_iota(jnp.int32, shape, 1)
            same = jnp.where(row // width == lane // width, 1.0 / width, 0.0)
            basis[:, pl.ds(level * columns, columns)] = same.astype(jnp.bfloat16)

    def block_means(step):
        shape = (8, columns)
        row = lax.broadcasted_iota(jnp.int32, shape, 0)
        for start in range(0, rings, 8):
            width = jnp.zeros(shape, jnp.int32)
            for ring in range(8):
                width = jnp.where(row == ring, width_smem[start + ring], width)
            values = jnp.concatenate(
                [
                    circle_increment[
                        block // planes,
                        block % planes,
                        pl.ds(start, 8),
                        pl.ds(sector * columns, columns),
                    ]
                    for block in range(blocks)
                    for sector in range(sectors)
                ],
                axis=0,
            )
            coarse = values.astype(jnp.bfloat16)
            fine = (values - coarse.astype(jnp.float32)).astype(jnp.bfloat16)
            means = jnp.dot(
                jnp.concatenate([coarse, fine], axis=1),
                basis[...],
                preferred_element_type=jnp.float32,
            )
            for block in range(blocks):
                picked, whole = [], []
                for sector in range(sectors):
                    first = (block * sectors + sector) * 8
                    mean = None
                    for level in range(level_count):
                        part = means[
                            first : first + 8, level * columns : (level + 1) * columns
                        ]
                        if mean is None:
                            mean = part
                        else:
                            mean = jnp.where(width == 2 << level, part, mean)
                    whole.append(part)
                    picked.append(mean)
                size = 2
                while size <= sectors:
                    for sector in range(sectors):
                        total = jnp.zeros(shape, jnp.float32)
                        for other in range(sectors):
                            if size == sectors:
                                total = total + whole[other]
                            else:
                                same = (az + sector) % sectors // size == (
                                    az + other
                                ) % sectors // size
                                total = total + jnp.where(same, 1.0, 0.0) * whole[other]
                        picked[sector] = jnp.where(
                            width == size * columns, total * (1.0 / size), picked[sector]
                        )
                    size *= 2
                c, plane = block // planes, block % planes
                here = pl.ds(PAD + start, 8)
                for sector in range(sectors):
                    lanes = pl.ds(sector * columns, columns)
                    if step == STEPS - 1 and sector > 0:
                        continue
                    value = circle[step, c, plane, here, lanes] + picked[sector]
                    if step == STEPS - 1:
                        out_ref[c, plane, pl.ds(start, 8)] = value
                    else:
                        circle[step + 1, c, plane, here, lanes] = value
                        if sector == 0:
                            state[step + 1, c, plane, here] = value

    off_axis = jnp.logical_not(at_axis)

    @pl.when(at_axis)
    def _():
        send_circle(0)
        for shift in range(1, sectors):
            gather(shift).start()

    @pl.when(off_axis)
    def _():
        send_planes(0, 0)

    for chunk in range(1, chunks):
        send_planes(0, chunk)

    @pl.when(jnp.logical_not(has_low))
    def _():
        low_plane[...] = jnp.zeros(low_plane.shape, jnp.float32)
        circle_low[...] = jnp.zeros(circle_low.shape, jnp.float32)

    @pl.when(jnp.logical_not(has_high))
    def _():
        high_plane[...] = jnp.zeros(high_plane.shape, jnp.float32)
        circle_high[...] = jnp.zeros(circle_high.shape, jnp.float32)

    load.wait()
    send_last_row(0)

    @pl.when(off_axis)
    def _():
        send_first_row(0)
        send_edges(0, 0)

    for chunk in range(1, chunks):
        send_edges(0, chunk)

    @pl.when(at_axis)
    def _():
        make_basis()

    load_width.wait()
    for step in range(STEPS):
        last = step == STEPS - 1
        receive_rows(step)

        @pl.when(at_axis)
        def _():
            in_circle(step)
            receive_circle(step)
            add_circle(step)
            block_means(step)
            if not last:
                send_circle(step + 1)

        @pl.when(off_axis)
        def _():
            in_plane(step, 0)

        for chunk in range(1, chunks):
            in_plane(step, chunk)

        @pl.when(off_axis)
        def _():
            receive_planes(step, 0)
            add_planes(step, 0)
            store(step, 0)
            if not last:
                send_planes(step + 1, 0)
                send_edges(step + 1, 0)
                send_first_row(step + 1)

        for chunk in range(1, chunks):
            receive_planes(step, chunk)
            add_planes(step, chunk)
            store(step, chunk)
            if not last:
                send_planes(step + 1, chunk)
                send_edges(step + 1, chunk)
                if chunk == 1:

                    @pl.when(at_axis)
                    def _():
                        send_rim(step + 1)

                if chunk == chunks - 1:
                    send_last_row(step + 1)

    @pl.when(off_axis)
    def _():
        load_circle.wait()

    for step in range(STEPS):
        for chunk in range(chunks):

            def sent():
                @pl.when(has_low)
                def _():
                    to_low(step, chunk).wait_send()

                @pl.when(has_high)
                def _():
                    to_high(step, chunk).wait_send()

                to_right(step, chunk).wait_send()
                if sectors > 2:
                    to_left(step, chunk).wait_send()

            if chunk == 0:
                pl.when(off_axis)(sent)
            else:
                sent()

        @pl.when(has_inner)
        def _():
            to_inner(step).wait_send()

        @pl.when(has_outer)
        def _():
            to_outer(step).wait_send()

        @pl.when(at_axis)
        def _():
            @pl.when(has_low)
            def _():
                circle_to_low(step).wait_send()
                if step == 0:
                    for shift in range(1, sectors):
                        corner_to_low(shift).wait_send()

            @pl.when(has_high)
            def _():
                circle_to_high(step).wait_send()
                if step == 0:
                    for shift in range(1, sectors):
                        corner_to_high(shift).wait_send()

            for shift in range(1, sectors):
                if step == 0:
                    gather(shift).wait_send()
                else:
                    to_rim(step, shift).wait_send()


def local(sizes, flow_state, cycle_widths):
    channels, planes, rows, columns = flow_state.shape
    rings = cycle_widths.shape[0]
    sectors = sizes[1]
    middle = rings + ((rows - rings) // 2 + 7) // 8 * 8
    bounds = (0, rings, middle, rows)
    chunks = len(bounds) - 1
    blocks = channels * planes
    around = sectors * columns
    f32 = jnp.float32
    dma = pltpu.SemaphoreType.DMA
    return pl.pallas_call(
        functools.partial(kernel, sizes, bounds),
        out_shape=pltpu.VMEM(flow_state.shape, f32),
        in_specs=[
            pl.BlockSpec(memory_space=pl.ANY),
            pl.BlockSpec(memory_space=pl.ANY),
        ],
        out_specs=pl.BlockSpec(memory_space=pltpu.VMEM),
        scratch_shapes=[
            pltpu.VMEM((STEPS, channels, planes, rows + 2 * PAD, columns), f32),
            pltpu.VMEM((channels, planes, rows, columns), f32),
            pltpu.VMEM((planes, rows, columns), f32),
            pltpu.VMEM((STEPS, channels, rows, columns), f32),
            pltpu.VMEM((STEPS, channels, rows, columns), f32),
            pltpu.VMEM((STEPS, rows, columns), f32),
            pltpu.VMEM((STEPS, rows, columns), f32),
            pltpu.VMEM((STEPS, rows, columns), f32),
            pltpu.VMEM((STEPS, 2, blocks, columns), f32),
            pltpu.VMEM((STEPS, 2, blocks, columns), f32),
            pltpu.VMEM((STEPS, channels, planes, rings + 2 * PAD, around), f32),
            pltpu.VMEM((channels, planes, rings, around), f32),
            pltpu.VMEM((planes, rings, around), f32),
            pltpu.VMEM((STEPS, channels, rings, around), f32),
            pltpu.VMEM((STEPS, channels, rings, around), f32),
            pltpu.VMEM((STEPS, sectors - 1, blocks, columns), f32),
            pltpu.VMEM((2 * columns, (columns.bit_length() - 1) * columns), jnp.bfloat16),
            pltpu.SMEM((rings,), jnp.int32),
            dma,
            dma,
            dma,
            dma((STEPS, chunks)),
            dma((STEPS, chunks)),
            dma((STEPS, chunks)),
            dma((STEPS, chunks)),
            dma((STEPS, chunks)),
            dma((STEPS, chunks)),
            dma((STEPS, chunks)),
            dma((STEPS, chunks)),
            dma((STEPS, 2)),
            dma((STEPS, 2)),
            dma((sectors - 1,)),
            dma((sectors - 1,)),
            dma((sectors - 1,)),
            dma((sectors - 1,)),
            dma((sectors - 1,)),
            dma((sectors - 1,)),
            dma((STEPS, sectors - 1)),
            dma((STEPS, sectors - 1)),
        ],
        compiler_params=pltpu.CompilerParams(
            collective_id=0, has_side_effects=True, vmem_limit_bytes=64 * 1024 * 1024 - 262144
        ),
    )(flow_state, cycle_widths)


def solution(mesh):
    sizes = (mesh.shape["ax"], mesh.shape["az"], mesh.shape["rad"])
    return jax.shard_map(
        functools.partial(local, sizes),
        mesh=mesh,
        in_specs=(P(None, ("groups", "ax"), "rad", "az"), P()),
        out_specs=P(None, ("groups", "ax"), "rad", "az"),
        check_vma=False,
    )
```

```python
import functools
import math

import jax
import jax.numpy as jnp
from jax import lax
from jax.experimental import pallas as pl
from jax.experimental.pallas import tpu as pltpu
from jax.sharding import PartitionSpec as P

STEPS = 2
DT = 0.2
KAPPA = 0.05
VISC = 0.1
RHO_RATIO = 20.0
PAD = 8
MESH = pl.DeviceIdType.MESH


def kernel(
    sizes,
    bounds,
    flow_ref,
    width_ref,
    out_ref,
    state,
    increment,
    spread,
    low_plane,
    high_plane,
    edge_out,
    edge_left,
    edge_right,
    row_out,
    row_in,
    circle,
    circle_increment,
    circle_spread,
    circle_low,
    circle_high,
    rim_in,
    basis,
    width_smem,
    load_sem,
    width_sem,
    circle_sem,
    low_send,
    low_recv,
    high_send,
    high_recv,
    left_send,
    left_recv,
    right_send,
    right_recv,
    row_send,
    row_recv,
    gather_send,
    gather_recv,
    corner_low_send,
    corner_low_recv,
    corner_high_send,
    corner_high_recv,
    rim_send,
    rim_recv,
):
    axials, sectors, rads = sizes
    channels, planes, rows, columns = flow_ref.shape
    blocks = channels * planes
    rings = width_ref.shape[0]
    around = sectors * columns
    chunks = len(bounds) - 1
    ax = lax.axis_index("ax")
    az = lax.axis_index("az")
    rad = lax.axis_index("rad")
    angle_step = 2.0 * math.pi / (sectors * columns)
    half_arc = DT / (2.0 * angle_step)
    has_low = ax > 0
    has_high = ax < axials - 1
    has_inner = rad > 0
    has_outer = rad < rads - 1
    at_axis = rad == 0
    left = (az + sectors - 1) % sectors
    right = (az + 1) % sectors

    load = pltpu.make_async_copy(
        flow_ref, state.at[0, :, :, pl.ds(PAD, rows)], load_sem
    )
    load.start()
    load_width = pltpu.make_async_copy(width_ref, width_smem, width_sem)
    load_width.start()
    load_circle = pltpu.make_async_copy(
        flow_ref.at[:, :, pl.ds(0, rings + 8)],
        circle.at[0, :, :, pl.ds(PAD, rings + 8), pl.ds(0, columns)],
        circle_sem,
    )
    load_circle.start()

    barrier = pltpu.get_barrier_semaphore()

    def greet(axis, place):
        pl.semaphore_signal(barrier, inc=1, device_id={axis: place}, device_id_type=MESH)

    def greet_corner(place, shift):
        pl.semaphore_signal(
            barrier,
            inc=1,
            device_id={"ax": place, "az": (az + shift) % sectors},
            device_id_type=MESH,
        )

    @pl.when(has_low)
    def _():
        greet("ax", ax - 1)

    @pl.when(has_high)
    def _():
        greet("ax", ax + 1)

    @pl.when(has_inner)
    def _():
        greet("rad", rad - 1)

    @pl.when(has_outer)
    def _():
        greet("rad", rad + 1)

    for shift in range(1, sectors):
        greet("az", (az + shift) % sectors)

    @pl.when(jnp.logical_and(at_axis, has_low))
    def _():
        for shift in range(1, sectors):
            greet_corner(ax - 1, shift)

    @pl.when(jnp.logical_and(at_axis, has_high))
    def _():
        for shift in range(1, sectors):
            greet_corner(ax + 1, shift)

    def one(flag):
        return jnp.where(flag, 1, 0)

    pl.semaphore_wait(
        barrier,
        one(has_low)
        + one(has_high)
        + one(has_inner)
        + one(has_outer)
        + sectors
        - 1
        + one(at_axis) * (one(has_low) + one(has_high)) * (sectors - 1),
    )

    def remote(src, dst, send, recv, axis, place):
        return pltpu.make_async_remote_copy(
            src_ref=src,
            dst_ref=dst,
            send_sem=send,
            recv_sem=recv,
            device_id={axis: place},
            device_id_type=MESH,
        )

    def span(chunk):
        return pl.ds(bounds[chunk], bounds[chunk + 1] - bounds[chunk])

    def own(chunk):
        return pl.ds(PAD + bounds[chunk], bounds[chunk + 1] - bounds[chunk])

    def source(step, plane, chunk):
        if step == 0:
            return flow_ref.at[:, plane, span(chunk)]
        return state.at[step, :, plane, own(chunk)]

    def to_low(step, chunk):
        return remote(
            source(step, 0, chunk),
            high_plane.at[step, :, span(chunk)],
            low_send.at[step, chunk],
            low_recv.at[step, chunk],
            "ax",
            ax - 1,
        )

    def to_high(step, chunk):
        return remote(
            source(step, planes - 1, chunk),
            low_plane.at[step, :, span(chunk)],
            high_send.at[step, chunk],
            high_recv.at[step, chunk],
            "ax",
            ax + 1,
        )

    def to_right(step, chunk):
        return remote(
            edge_out.at[step, span(chunk)],
            edge_left.at[step, span(chunk)],
            right_send.at[step, chunk],
            right_recv.at[step, chunk],
            "az",
            right,
        )

    def to_left(step, chunk):
        return remote(
            edge_out.at[step, span(chunk)],
            edge_right.at[step, span(chunk)],
            left_send.at[step, chunk],
            left_recv.at[step, chunk],
            "az",
            left,
        )

    def to_inner(step):
        return remote(
            row_out.at[step, 0],
            row_in.at[step, 1],
            row_send.at[step, 0],
            row_recv.at[step, 0],
            "rad",
            rad - 1,
        )

    def to_outer(step):
        return remote(
            row_out.at[step, 1],
            row_in.at[step, 0],
            row_send.at[step, 1],
            row_recv.at[step, 1],
            "rad",
            rad + 1,
        )

    def circle_source(step, plane):
        if step == 0:
            return flow_ref.at[:, plane, pl.ds(0, rings)]
        return circle.at[step, :, plane, pl.ds(PAD, rings)]

    def circle_target(ref, step):
        if step == 0:
            return ref.at[step, :, :, pl.ds(0, columns)]
        return ref.at[step]

    def circle_to_low(step):
        return remote(
            circle_source(step, 0),
            circle_target(circle_high, step),
            low_send.at[step, 0],
            low_recv.at[step, 0],
            "ax",
            ax - 1,
        )

    def circle_to_high(step):
        return remote(
            circle_source(step, planes - 1),
            circle_target(circle_low, step),
            high_send.at[step, 0],
            high_recv.at[step, 0],
            "ax",
            ax + 1,
        )

    def corner_to_low(shift):
        return pltpu.make_async_remote_copy(
            src_ref=flow_ref.at[:, 0, pl.ds(0, rings)],
            dst_ref=circle_high.at[0, :, :, pl.ds((sectors - shift) * columns, columns)],
            send_sem=corner_low_send.at[shift - 1],
            recv_sem=corner_low_recv.at[shift - 1],
            device_id={"ax": ax - 1, "az": (az + shift) % sectors},
            device_id_type=MESH,
        )

    def corner_to_high(shift):
        return pltpu.make_async_remote_copy(
            src_ref=flow_ref.at[:, planes - 1, pl.ds(0, rings)],
            dst_ref=circle_low.at[0, :, :, pl.ds((sectors - shift) * columns, columns)],
            send_sem=corner_high_send.at[shift - 1],
            recv_sem=corner_high_recv.at[shift - 1],
            device_id={"ax": ax + 1, "az": (az + shift) % sectors},
            device_id_type=MESH,
        )

    def gather(shift):
        return remote(
            flow_ref.at[:, :, pl.ds(0, rings + 8)],
            circle.at[
                0, :, :, pl.ds(PAD, rings + 8), pl.ds((sectors - shift) * columns, columns)
            ],
            gather_send.at[shift - 1],
            gather_recv.at[shift - 1],
            "az",
            (az + shift) % sectors,
        )

    def to_rim(step, shift):
        return remote(
            row_out.at[step, 0],
            rim_in.at[step, sectors - shift - 1],
            rim_send.at[step, shift - 1],
            rim_recv.at[step, shift - 1],
            "az",
            (az + shift) % sectors,
        )

    def send_circle(step):
        @pl.when(has_low)
        def _():
            circle_to_low(step).start()
            if step == 0:
                for shift in range(1, sectors):
                    corner_to_low(shift).start()

        @pl.when(has_high)
        def _():
            circle_to_high(step).start()
            if step == 0:
                for shift in range(1, sectors):
                    corner_to_high(shift).start()

    def receive_circle(step):
        @pl.when(has_low)
        def _():
            circle_to_high(step).wait_recv()
            if step == 0:
                for shift in range(1, sectors):
                    corner_to_high(shift).wait_recv()

        @pl.when(has_high)
        def _():
            circle_to_low(step).wait_recv()
            if step == 0:
                for shift in range(1, sectors):
                    corner_to_low(shift).wait_recv()

    def send_rim(step):
        for block in range(blocks):
            row = state[step, block // planes, block % planes, pl.ds(PAD + rings, 1)]
            row_out[step, 0, pl.ds(block, 1)] = row
            circle[
                step, block // planes, block % planes, pl.ds(PAD + rings, 1), pl.ds(0, columns)
            ] = row
        for shift in range(1, sectors):
            to_rim(step, shift).start()

    def receive_rim(step):
        for shift in range(1, sectors):
            to_rim(step, shift).wait_recv()
            place = sectors - shift
            for block in range(blocks):
                circle[
                    step,
                    block // planes,
                    block % planes,
                    pl.ds(PAD + rings, 1),
                    pl.ds(place * columns, columns),
                ] = rim_in[step, place - 1, pl.ds(block, 1)]

    def send_planes(step, chunk):
        @pl.when(has_low)
        def _():
            to_low(step, chunk).start()

        @pl.when(has_high)
        def _():
            to_high(step, chunk).start()

    def send_edges(step, chunk):
        count = bounds[chunk + 1] - bounds[chunk]
        lane = lax.broadcasted_iota(jnp.int32, (count, columns), 1)
        packed = jnp.zeros((count, columns), jnp.float32)
        for block in range(blocks):
            values = state[step, block // planes, block % planes, own(chunk)]
            packed = jnp.where(
                lane // 2 == block, pltpu.roll(values, 2 * block + 1, 1), packed
            )
        edge_out[step, span(chunk)] = packed
        to_right(step, chunk).start()
        if sectors > 2:
            to_left(step, chunk).start()

    def send_first_row(step):
        for block in range(blocks):
            row_out[step, 0, pl.ds(block, 1)] = state[
                step, block // planes, block % planes, pl.ds(PAD, 1)
            ]

        to_inner(step).start()

    def send_last_row(step):
        for block in range(blocks):
            row_out[step, 1, pl.ds(block, 1)] = state[
                step, block // planes, block % planes, pl.ds(PAD + rows - 1, 1)
            ]

        @pl.when(has_outer)
        def _():
            to_outer(step).start()

    def receive_rows(step):
        @pl.when(has_inner)
        def _():
            to_outer(step).wait_recv()
            for block in range(blocks):
                state[step, block // planes, block % planes, pl.ds(PAD - 1, 1)] = row_in[
                    step, 0, pl.ds(block, 1)
                ]

        @pl.when(has_outer)
        def _():
            to_inner(step).wait_recv()
            for block in range(blocks):
                state[step, block // planes, block % planes, pl.ds(PAD + rows, 1)] = row_in[
                    step, 1, pl.ds(block, 1)
                ]

        @pl.when(jnp.logical_not(has_outer))
        def _():
            for block in range(blocks):
                state[step, block // planes, block % planes, pl.ds(PAD + rows, 1)] = jnp.zeros(
                    (1, columns), jnp.float32
                )

    def terms(start, shape):
        row = lax.broadcasted_iota(jnp.int32, shape, 0)
        radius = (rad * rows + start + row).astype(jnp.float32) + 0.5
        reciprocal = 1.0 / radius
        return (
            reciprocal,
            half_arc * reciprocal,
            1.0 + 0.5 * reciprocal,
            1.0 - 0.5 * reciprocal,
            (0.5 * DT) * (1.0 + reciprocal),
            (0.5 * DT) * (1.0 - reciprocal),
        )

    def plane_rates(weights, center, outer, inner, ahead, behind, upper, lower):
        reciprocal, arc, outer_weight, inner_weight, outer_flux, inner_flux = weights
        level, axial, radial, swirl = center
        density = 1.0 + (RHO_RATIO - 1.0) * jnp.clip(level, 0.0, 1.0)
        thin = (DT * VISC) / density
        laplace = [
            outer_weight * outer[c] + inner_weight * inner[c] - 4.0 * center[c]
            for c in range(channels)
        ]
        for other in (upper, lower):
            if other is not None:
                laplace = [laplace[c] + other[c] for c in range(channels)]
        rate = (
            (DT * KAPPA) * laplace[0]
            - outer_flux * outer[2] * outer[0]
            + inner_flux * inner[2] * inner[0]
            - arc * (ahead[3] * ahead[0] - behind[3] * behind[0])
        )
        if upper is not None:
            rate = rate - (0.5 * DT) * upper[1] * upper[0]
        if lower is not None:
            rate = rate + (0.5 * DT) * lower[1] * lower[0]
        found = [rate]
        drift = (0.5 * DT) * axial
        push = (0.5 * DT) * radial
        turn = arc * swirl
        for c in range(1, channels):
            rate = (
                thin * laplace[c]
                - push * (outer[c] - inner[c])
                - turn * (ahead[c] - behind[c])
            )
            if upper is not None:
                rate = rate - drift * upper[c]
            if lower is not None:
                rate = rate + drift * lower[c]
            if c == 2:
                rate = rate + (DT * reciprocal) * swirl * swirl
            if c == 3:
                rate = rate - (DT * reciprocal) * swirl * radial
            found.append(rate)
        return thin, found

    def in_plane(step, chunk):
        to_right(step, chunk).wait_recv()
        if sectors > 2:
            to_left(step, chunk).wait_recv()
        for start in range(bounds[chunk], bounds[chunk + 1], 8):
            shape = (8, columns)
            lane = lax.broadcasted_iota(jnp.int32, shape, 1)
            weights = terms(start, shape)
            edges = edge_left[step, pl.ds(start, 8)]
            if sectors > 2:
                edges = jnp.where(lane % 2 == 0, edges, edge_right[step, pl.ds(start, 8)])

            def cell(channel, plane, offset=0):
                return state[step, channel, plane, pl.ds(PAD + start + offset, 8)]

            def cells(plane, offset=0):
                return [cell(c, plane, offset) for c in range(channels)]

            for plane in range(planes):
                center = cells(plane)
                ahead, behind = [], []
                for c in range(channels):
                    block = c * planes + plane
                    rim = pltpu.roll(edges, (columns - 2 * block - 1) % columns, 1)
                    ahead.append(
                        pltpu.roll(jnp.where(lane == 0, rim, center[c]), columns - 1, 1)
                    )
                    behind.append(
                        pltpu.roll(jnp.where(lane == columns - 1, rim, center[c]), 1, 1)
                    )
                thin, rate = plane_rates(
                    weights,
                    center,
                    cells(plane, 1),
                    cells(plane, -1),
                    ahead,
                    behind,
                    cells(plane + 1) if plane < planes - 1 else None,
                    cells(plane - 1) if plane > 0 else None,
                )
                spread[plane, pl.ds(start, 8)] = thin
                for c in range(channels):
                    increment[c, plane, pl.ds(start, 8)] = rate[c]

    def in_circle(step):
        if step == 0:
            load_circle.wait()
            for shift in range(1, sectors):
                gather(shift).wait_recv()
        else:
            receive_rim(step)
        for c in range(channels):
            sign = 1.0 if c < 2 else -1.0
            for plane in range(planes):
                first = circle[step, c, plane, pl.ds(PAD, 8)]
                circle[step, c, plane, pl.ds(PAD - 1, 1)] = (
                    sign * pltpu.roll(first, around // 2, 1)[:1]
                )
        for start in range(0, rings, 8):
            weights = terms(start, (8, around))

            def cells(plane, offset=0):
                return [
                    circle[step, c, plane, pl.ds(PAD + start + offset, 8)]
                    for c in range(channels)
                ]

            for plane in range(planes):
                center = cells(plane)
                thin, rate = plane_rates(
                    weights,
                    center,
                    cells(plane, 1),
                    cells(plane, -1),
                    [pltpu.roll(x, around - 1, 1) for x in center],
                    [pltpu.roll(x, 1, 1) for x in center],
                    cells(plane + 1) if plane < planes - 1 else None,
                    cells(plane - 1) if plane > 0 else None,
                )
                circle_spread[plane, pl.ds(start, 8)] = thin
                for c in range(channels):
                    circle_increment[c, plane, pl.ds(start, 8)] = rate[c]

    def receive_planes(step, chunk):
        @pl.when(has_low)
        def _():
            to_high(step, chunk).wait_recv()

        @pl.when(has_high)
        def _():
            to_low(step, chunk).wait_recv()

    def add_planes(step, chunk):
        for plane, halo, sign in ((0, low_plane, 1.0), (planes - 1, high_plane, -1.0)):
            here = span(chunk)
            drift = (sign * 0.5 * DT) * state[step, 1, plane, own(chunk)]
            weight = drift + spread[plane, here]
            level = halo[step, 0, here]
            increment[0, plane, here] += level * (
                DT * KAPPA + (sign * 0.5 * DT) * halo[step, 1, here]
            )
            for c in range(1, channels):
                increment[c, plane, here] += weight * halo[step, c, here]

    def store(step, chunk):
        for c in range(channels):
            for plane in range(planes):
                value = state[step, c, plane, own(chunk)] + increment[c, plane, span(chunk)]
                if step == STEPS - 1:
                    out_ref[c, plane, span(chunk)] = value
                else:
                    state[step + 1, c, plane, own(chunk)] = value

    def add_circle(step):
        for plane, halo, sign in ((0, circle_low, 1.0), (planes - 1, circle_high, -1.0)):
            drift = (sign * 0.5 * DT) * circle[step, 1, plane, pl.ds(PAD, rings)]
            weight = drift + circle_spread[plane]
            circle_increment[0, plane] += halo[step, 0] * (
                DT * KAPPA + (sign * 0.5 * DT) * halo[step, 1]
            )
            for c in range(1, channels):
                circle_increment[c, plane] += weight * halo[step, c]

    level_count = columns.bit_length() - 1

    def make_basis():
        for level in range(level_count):
            width = 2 << level
            shape = (2 * columns, columns)
            row = lax.broadcasted_iota(jnp.int32, shape, 0) % columns
            lane = lax.broadcasted_iota(jnp.int32, shape, 1)
            same = jnp.where(row // width == lane // width, 1.0 / width, 0.0)
            basis[:, pl.ds(level * columns, columns)] = same.astype(jnp.bfloat16)

    def block_means(step):
        shape = (8, columns)
        row = lax.broadcasted_iota(jnp.int32, shape, 0)
        for start in range(0, rings, 8):
            width = jnp.zeros(shape, jnp.int32)
            for ring in range(8):
                width = jnp.where(row == ring, width_smem[start + ring], width)
            values = jnp.concatenate(
                [
                    circle_increment[
                        block // planes,
                        block % planes,
                        pl.ds(start, 8),
                        pl.ds(sector * columns, columns),
                    ]
                    for block in range(blocks)
                    for sector in range(sectors)
                ],
                axis=0,
            )
            coarse = values.astype(jnp.bfloat16)
            fine = (values - coarse.astype(jnp.float32)).astype(jnp.bfloat16)
            means = jnp.dot(
                jnp.concatenate([coarse, fine], axis=1),
                basis[...],
                preferred_element_type=jnp.float32,
            )
            for block in range(blocks):
                picked, whole = [], []
                for sector in range(sectors):
                    first = (block * sectors + sector) * 8
                    mean = None
                    for level in range(level_count):
                        part = means[
                            first : first + 8, level * columns : (level + 1) * columns
                        ]
                        if mean is None:
                            mean = part
                        else:
                            mean = jnp.where(width == 2 << level, part, mean)
                    whole.append(part)
                    picked.append(mean)
                size = 2
                while size <= sectors:
                    for sector in range(sectors):
                        total = jnp.zeros(shape, jnp.float32)
                        for other in range(sectors):
                            if size == sectors:
                                total = total + whole[other]
                            else:
                                same = (az + sector) % sectors // size == (
                                    az + other
                                ) % sectors // size
                                total = total + jnp.where(same, 1.0, 0.0) * whole[other]
                        picked[sector] = jnp.where(
                            width == size * columns, total * (1.0 / size), picked[sector]
                        )
                    size *= 2
                c, plane = block // planes, block % planes
                here = pl.ds(PAD + start, 8)
                for sector in range(sectors):
                    lanes = pl.ds(sector * columns, columns)
                    if step == STEPS - 1 and sector > 0:
                        continue
                    value = circle[step, c, plane, here, lanes] + picked[sector]
                    if step == STEPS - 1:
                        out_ref[c, plane, pl.ds(start, 8)] = value
                    else:
                        circle[step + 1, c, plane, here, lanes] = value
                        if sector == 0:
                            state[step + 1, c, plane, here] = value

    off_axis = jnp.logical_not(at_axis)

    @pl.when(at_axis)
    def _():
        send_circle(0)
        for shift in range(1, sectors):
            gather(shift).start()

    @pl.when(off_axis)
    def _():
        send_planes(0, 0)

    for chunk in range(1, chunks):
        send_planes(0, chunk)

    @pl.when(jnp.logical_not(has_low))
    def _():
        low_plane[...] = jnp.zeros(low_plane.shape, jnp.float32)
        circle_low[...] = jnp.zeros(circle_low.shape, jnp.float32)

    @pl.when(jnp.logical_not(has_high))
    def _():
        high_plane[...] = jnp.zeros(high_plane.shape, jnp.float32)
        circle_high[...] = jnp.zeros(circle_high.shape, jnp.float32)

    load.wait()
    send_last_row(0)

    @pl.when(off_axis)
    def _():
        send_first_row(0)
        send_edges(0, 0)

    for chunk in range(1, chunks):
        send_edges(0, chunk)

    @pl.when(at_axis)
    def _():
        make_basis()

    load_width.wait()
    for step in range(STEPS):
        last = step == STEPS - 1
        receive_rows(step)

        @pl.when(at_axis)
        def _():
            in_circle(step)

        @pl.when(off_axis)
        def _():
            in_plane(step, 0)

        for chunk in range(1, chunks):
            in_plane(step, chunk)

        @pl.when(at_axis)
        def _():
            receive_circle(step)
            add_circle(step)
            block_means(step)
            if not last:
                send_circle(step + 1)

        @pl.when(off_axis)
        def _():
            receive_planes(step, 0)
            add_planes(step, 0)
            store(step, 0)
            if not last:
                send_planes(step + 1, 0)
                send_edges(step + 1, 0)
                send_first_row(step + 1)

        for chunk in range(1, chunks):
            receive_planes(step, chunk)
            add_planes(step, chunk)
            store(step, chunk)
            if not last:
                send_planes(step + 1, chunk)
                send_edges(step + 1, chunk)
                if chunk == 1:

                    @pl.when(at_axis)
                    def _():
                        send_rim(step + 1)

                if chunk == chunks - 1:
                    send_last_row(step + 1)

    @pl.when(off_axis)
    def _():
        load_circle.wait()

    for step in range(STEPS):
        for chunk in range(chunks):

            def sent():
                @pl.when(has_low)
                def _():
                    to_low(step, chunk).wait_send()

                @pl.when(has_high)
                def _():
                    to_high(step, chunk).wait_send()

                to_right(step, chunk).wait_send()
                if sectors > 2:
                    to_left(step, chunk).wait_send()

            if chunk == 0:
                pl.when(off_axis)(sent)
            else:
                sent()

        @pl.when(has_inner)
        def _():
            to_inner(step).wait_send()

        @pl.when(has_outer)
        def _():
            to_outer(step).wait_send()

        @pl.when(at_axis)
        def _():
            @pl.when(has_low)
            def _():
                circle_to_low(step).wait_send()
                if step == 0:
                    for shift in range(1, sectors):
                        corner_to_low(shift).wait_send()

            @pl.when(has_high)
            def _():
                circle_to_high(step).wait_send()
                if step == 0:
                    for shift in range(1, sectors):
                        corner_to_high(shift).wait_send()

            for shift in range(1, sectors):
                if step == 0:
                    gather(shift).wait_send()
                else:
                    to_rim(step, shift).wait_send()


def local(sizes, flow_state, cycle_widths):
    channels, planes, rows, columns = flow_state.shape
    rings = cycle_widths.shape[0]
    sectors = sizes[1]
    middle = rings + ((rows - rings) // 2 + 7) // 8 * 8
    bounds = (0, rings, middle, rows)
    chunks = len(bounds) - 1
    blocks = channels * planes
    around = sectors * columns
    f32 = jnp.float32
    dma = pltpu.SemaphoreType.DMA
    return pl.pallas_call(
        functools.partial(kernel, sizes, bounds),
        out_shape=pltpu.VMEM(flow_state.shape, f32),
        in_specs=[
            pl.BlockSpec(memory_space=pl.ANY),
            pl.BlockSpec(memory_space=pl.ANY),
        ],
        out_specs=pl.BlockSpec(memory_space=pltpu.VMEM),
        scratch_shapes=[
            pltpu.VMEM((STEPS, channels, planes, rows + 2 * PAD, columns), f32),
            pltpu.VMEM((channels, planes, rows, columns), f32),
            pltpu.VMEM((planes, rows, columns), f32),
            pltpu.VMEM((STEPS, channels, rows, columns), f32),
            pltpu.VMEM((STEPS, channels, rows, columns), f32),
            pltpu.VMEM((STEPS, rows, columns), f32),
            pltpu.VMEM((STEPS, rows, columns), f32),
            pltpu.VMEM((STEPS, rows, columns), f32),
            pltpu.VMEM((STEPS, 2, blocks, columns), f32),
            pltpu.VMEM((STEPS, 2, blocks, columns), f32),
            pltpu.VMEM((STEPS, channels, planes, rings + 2 * PAD, around), f32),
            pltpu.VMEM((channels, planes, rings, around), f32),
            pltpu.VMEM((planes, rings, around), f32),
            pltpu.VMEM((STEPS, channels, rings, around), f32),
            pltpu.VMEM((STEPS, channels, rings, around), f32),
            pltpu.VMEM((STEPS, sectors - 1, blocks, columns), f32),
            pltpu.VMEM((2 * columns, (columns.bit_length() - 1) * columns), jnp.bfloat16),
            pltpu.SMEM((rings,), jnp.int32),
            dma,
            dma,
            dma,
            dma((STEPS, chunks)),
            dma((STEPS, chunks)),
            dma((STEPS, chunks)),
            dma((STEPS, chunks)),
            dma((STEPS, chunks)),
            dma((STEPS, chunks)),
            dma((STEPS, chunks)),
            dma((STEPS, chunks)),
            dma((STEPS, 2)),
            dma((STEPS, 2)),
            dma((sectors - 1,)),
            dma((sectors - 1,)),
            dma((sectors - 1,)),
            dma((sectors - 1,)),
            dma((sectors - 1,)),
            dma((sectors - 1,)),
            dma((STEPS, sectors - 1)),
            dma((STEPS, sectors - 1)),
        ],
        compiler_params=pltpu.CompilerParams(
            collective_id=0, has_side_effects=True, vmem_limit_bytes=64 * 1024 * 1024 - 262144
        ),
    )(flow_state, cycle_widths)


def solution(mesh):
    sizes = (mesh.shape["ax"], mesh.shape["az"], mesh.shape["rad"])
    return jax.shard_map(
        functools.partial(local, sizes),
        mesh=mesh,
        in_specs=(P(None, ("groups", "ax"), "rad", "az"), P()),
        out_specs=P(None, ("groups", "ax"), "rad", "az"),
        check_vma=False,
    )
```

```python
import functools
import math

import jax
import jax.numpy as jnp
from jax import lax
from jax.experimental import pallas as pl
from jax.experimental.pallas import tpu as pltpu
from jax.sharding import PartitionSpec as P

STEPS = 2
DT = 0.2
KAPPA = 0.05
VISC = 0.1
RHO_RATIO = 20.0
PAD = 8
MESH = pl.DeviceIdType.MESH


def kernel(
    sizes,
    bounds,
    flow_ref,
    width_ref,
    out_ref,
    state,
    increment,
    spread,
    low_plane,
    high_plane,
    edge_out,
    edge_left,
    edge_right,
    row_out,
    row_in,
    circle,
    circle_increment,
    circle_spread,
    circle_low,
    circle_high,
    rim_in,
    basis,
    width_smem,
    load_sem,
    width_sem,
    circle_sem,
    low_send,
    low_recv,
    high_send,
    high_recv,
    left_send,
    left_recv,
    right_send,
    right_recv,
    row_send,
    row_recv,
    gather_send,
    gather_recv,
    corner_low_send,
    corner_low_recv,
    corner_high_send,
    corner_high_recv,
    rim_send,
    rim_recv,
):
    axials, sectors, rads = sizes
    channels, planes, rows, columns = flow_ref.shape
    blocks = channels * planes
    rings = width_ref.shape[0]
    around = sectors * columns
    chunks = len(bounds) - 1
    ax = lax.axis_index("ax")
    az = lax.axis_index("az")
    rad = lax.axis_index("rad")
    angle_step = 2.0 * math.pi / (sectors * columns)
    half_arc = DT / (2.0 * angle_step)
    has_low = ax > 0
    has_high = ax < axials - 1
    has_inner = rad > 0
    has_outer = rad < rads - 1
    at_axis = rad == 0
    left = (az + sectors - 1) % sectors
    right = (az + 1) % sectors

    load = pltpu.make_async_copy(
        flow_ref, state.at[0, :, :, pl.ds(PAD, rows)], load_sem
    )
    load.start()
    load_width = pltpu.make_async_copy(width_ref, width_smem, width_sem)
    load_width.start()
    load_circle = pltpu.make_async_copy(
        flow_ref.at[:, :, pl.ds(0, rings + 8)],
        circle.at[0, :, :, pl.ds(PAD, rings + 8), pl.ds(0, columns)],
        circle_sem,
    )
    load_circle.start()

    barrier = pltpu.get_barrier_semaphore()

    def greet(axis, place):
        pl.semaphore_signal(barrier, inc=1, device_id={axis: place}, device_id_type=MESH)

    def greet_corner(place, shift):
        pl.semaphore_signal(
            barrier,
            inc=1,
            device_id={"ax": place, "az": (az + shift) % sectors},
            device_id_type=MESH,
        )

    @pl.when(has_low)
    def _():
        greet("ax", ax - 1)

    @pl.when(has_high)
    def _():
        greet("ax", ax + 1)

    @pl.when(has_inner)
    def _():
        greet("rad", rad - 1)

    @pl.when(has_outer)
    def _():
        greet("rad", rad + 1)

    for shift in range(1, sectors):
        greet("az", (az + shift) % sectors)

    @pl.when(jnp.logical_and(at_axis, has_low))
    def _():
        for shift in range(1, sectors):
            greet_corner(ax - 1, shift)

    @pl.when(jnp.logical_and(at_axis, has_high))
    def _():
        for shift in range(1, sectors):
            greet_corner(ax + 1, shift)

    def one(flag):
        return jnp.where(flag, 1, 0)

    pl.semaphore_wait(
        barrier,
        one(has_low)
        + one(has_high)
        + one(has_inner)
        + one(has_outer)
        + sectors
        - 1
        + one(at_axis) * (one(has_low) + one(has_high)) * (sectors - 1),
    )

    def remote(src, dst, send, recv, axis, place):
        return pltpu.make_async_remote_copy(
            src_ref=src,
            dst_ref=dst,
            send_sem=send,
            recv_sem=recv,
            device_id={axis: place},
            device_id_type=MESH,
        )

    def span(chunk):
        return pl.ds(bounds[chunk], bounds[chunk + 1] - bounds[chunk])

    def own(chunk):
        return pl.ds(PAD + bounds[chunk], bounds[chunk + 1] - bounds[chunk])

    def source(step, plane, chunk):
        if step == 0:
            return flow_ref.at[:, plane, span(chunk)]
        return state.at[step, :, plane, own(chunk)]

    def to_low(step, chunk):
        return remote(
            source(step, 0, chunk),
            high_plane.at[step, :, span(chunk)],
            low_send.at[step, chunk],
            low_recv.at[step, chunk],
            "ax",
            ax - 1,
        )

    def to_high(step, chunk):
        return remote(
            source(step, planes - 1, chunk),
            low_plane.at[step, :, span(chunk)],
            high_send.at[step, chunk],
            high_recv.at[step, chunk],
            "ax",
            ax + 1,
        )

    def to_right(step, chunk):
        return remote(
            edge_out.at[step, span(chunk)],
            edge_left.at[step, span(chunk)],
            right_send.at[step, chunk],
            right_recv.at[step, chunk],
            "az",
            right,
        )

    def to_left(step, chunk):
        return remote(
            edge_out.at[step, span(chunk)],
            edge_right.at[step, span(chunk)],
            left_send.at[step, chunk],
            left_recv.at[step, chunk],
            "az",
            left,
        )

    def to_inner(step):
        return remote(
            row_out.at[step, 0],
            row_in.at[step, 1],
            row_send.at[step, 0],
            row_recv.at[step, 0],
            "rad",
            rad - 1,
        )

    def to_outer(step):
        return remote(
            row_out.at[step, 1],
            row_in.at[step, 0],
            row_send.at[step, 1],
            row_recv.at[step, 1],
            "rad",
            rad + 1,
        )

    def circle_source(step, plane):
        if step == 0:
            return flow_ref.at[:, plane, pl.ds(0, rings)]
        return circle.at[step, :, plane, pl.ds(PAD, rings)]

    def circle_target(ref, step):
        if step == 0:
            return ref.at[step, :, :, pl.ds(0, columns)]
        return ref.at[step]

    def circle_to_low(step):
        return remote(
            circle_source(step, 0),
            circle_target(circle_high, step),
            low_send.at[step, 0],
            low_recv.at[step, 0],
            "ax",
            ax - 1,
        )

    def circle_to_high(step):
        return remote(
            circle_source(step, planes - 1),
            circle_target(circle_low, step),
            high_send.at[step, 0],
            high_recv.at[step, 0],
            "ax",
            ax + 1,
        )

    def corner_to_low(shift):
        return pltpu.make_async_remote_copy(
            src_ref=flow_ref.at[:, 0, pl.ds(0, rings)],
            dst_ref=circle_high.at[0, :, :, pl.ds((sectors - shift) * columns, columns)],
            send_sem=corner_low_send.at[shift - 1],
            recv_sem=corner_low_recv.at[shift - 1],
            device_id={"ax": ax - 1, "az": (az + shift) % sectors},
            device_id_type=MESH,
        )

    def corner_to_high(shift):
        return pltpu.make_async_remote_copy(
            src_ref=flow_ref.at[:, planes - 1, pl.ds(0, rings)],
            dst_ref=circle_low.at[0, :, :, pl.ds((sectors - shift) * columns, columns)],
            send_sem=corner_high_send.at[shift - 1],
            recv_sem=corner_high_recv.at[shift - 1],
            device_id={"ax": ax + 1, "az": (az + shift) % sectors},
            device_id_type=MESH,
        )

    def gather(shift):
        return remote(
            flow_ref.at[:, :, pl.ds(0, rings + 8)],
            circle.at[
                0, :, :, pl.ds(PAD, rings + 8), pl.ds((sectors - shift) * columns, columns)
            ],
            gather_send.at[shift - 1],
            gather_recv.at[shift - 1],
            "az",
            (az + shift) % sectors,
        )

    def to_rim(step, shift):
        return remote(
            row_out.at[step, 0],
            rim_in.at[step, sectors - shift - 1],
            rim_send.at[step, shift - 1],
            rim_recv.at[step, shift - 1],
            "az",
            (az + shift) % sectors,
        )

    def send_circle(step):
        @pl.when(has_low)
        def _():
            circle_to_low(step).start()
            if step == 0:
                for shift in range(1, sectors):
                    corner_to_low(shift).start()

        @pl.when(has_high)
        def _():
            circle_to_high(step).start()
            if step == 0:
                for shift in range(1, sectors):
                    corner_to_high(shift).start()

    def receive_circle(step):
        @pl.when(has_low)
        def _():
            circle_to_high(step).wait_recv()
            if step == 0:
                for shift in range(1, sectors):
                    corner_to_high(shift).wait_recv()

        @pl.when(has_high)
        def _():
            circle_to_low(step).wait_recv()
            if step == 0:
                for shift in range(1, sectors):
                    corner_to_low(shift).wait_recv()

    def send_rim(step):
        for block in range(blocks):
            row = state[step, block // planes, block % planes, pl.ds(PAD + rings, 1)]
            row_out[step, 0, pl.ds(block, 1)] = row
            circle[
                step, block // planes, block % planes, pl.ds(PAD + rings, 1), pl.ds(0, columns)
            ] = row
        for shift in range(1, sectors):
            to_rim(step, shift).start()

    def receive_rim(step):
        for shift in range(1, sectors):
            to_rim(step, shift).wait_recv()
            place = sectors - shift
            for block in range(blocks):
                circle[
                    step,
                    block // planes,
                    block % planes,
                    pl.ds(PAD + rings, 1),
                    pl.ds(place * columns, columns),
                ] = rim_in[step, place - 1, pl.ds(block, 1)]

    def send_planes(step, chunk):
        @pl.when(has_low)
        def _():
            to_low(step, chunk).start()

        @pl.when(has_high)
        def _():
            to_high(step, chunk).start()

    def send_edges(step, chunk):
        count = bounds[chunk + 1] - bounds[chunk]
        lane = lax.broadcasted_iota(jnp.int32, (count, columns), 1)
        packed = jnp.zeros((count, columns), jnp.float32)
        for block in range(blocks):
            values = state[step, block // planes, block % planes, own(chunk)]
            packed = jnp.where(
                lane // 2 == block, pltpu.roll(values, 2 * block + 1, 1), packed
            )
        edge_out[step, span(chunk)] = packed
        to_right(step, chunk).start()
        if sectors > 2:
            to_left(step, chunk).start()

    def send_first_row(step):
        for block in range(blocks):
            row_out[step, 0, pl.ds(block, 1)] = state[
                step, block // planes, block % planes, pl.ds(PAD, 1)
            ]

        to_inner(step).start()

    def send_last_row(step):
        for block in range(blocks):
            row_out[step, 1, pl.ds(block, 1)] = state[
                step, block // planes, block % planes, pl.ds(PAD + rows - 1, 1)
            ]

        @pl.when(has_outer)
        def _():
            to_outer(step).start()

    def receive_rows(step):
        @pl.when(has_inner)
        def _():
            to_outer(step).wait_recv()
            for block in range(blocks):
                state[step, block // planes, block % planes, pl.ds(PAD - 1, 1)] = row_in[
                    step, 0, pl.ds(block, 1)
                ]

        @pl.when(has_outer)
        def _():
            to_inner(step).wait_recv()
            for block in range(blocks):
                state[step, block // planes, block % planes, pl.ds(PAD + rows, 1)] = row_in[
                    step, 1, pl.ds(block, 1)
                ]

        @pl.when(jnp.logical_not(has_outer))
        def _():
            for block in range(blocks):
                state[step, block // planes, block % planes, pl.ds(PAD + rows, 1)] = jnp.zeros(
                    (1, columns), jnp.float32
                )

    def terms(start, shape):
        row = lax.broadcasted_iota(jnp.int32, shape, 0)
        radius = (rad * rows + start + row).astype(jnp.float32) + 0.5
        reciprocal = 1.0 / radius
        return (
            reciprocal,
            half_arc * reciprocal,
            1.0 + 0.5 * reciprocal,
            1.0 - 0.5 * reciprocal,
            (0.5 * DT) * (1.0 + reciprocal),
            (0.5 * DT) * (1.0 - reciprocal),
        )

    def plane_rates(weights, center, outer, inner, ahead, behind, upper, lower):
        reciprocal, arc, outer_weight, inner_weight, outer_flux, inner_flux = weights
        level, axial, radial, swirl = center
        density = 1.0 + (RHO_RATIO - 1.0) * jnp.clip(level, 0.0, 1.0)
        thin = (DT * VISC) / density
        laplace = [
            outer_weight * outer[c] + inner_weight * inner[c] - 4.0 * center[c]
            for c in range(channels)
        ]
        for other in (upper, lower):
            if other is not None:
                laplace = [laplace[c] + other[c] for c in range(channels)]
        rate = (
            (DT * KAPPA) * laplace[0]
            - outer_flux * outer[2] * outer[0]
            + inner_flux * inner[2] * inner[0]
            - arc * (ahead[3] * ahead[0] - behind[3] * behind[0])
        )
        if upper is not None:
            rate = rate - (0.5 * DT) * upper[1] * upper[0]
        if lower is not None:
            rate = rate + (0.5 * DT) * lower[1] * lower[0]
        found = [rate]
        drift = (0.5 * DT) * axial
        push = (0.5 * DT) * radial
        turn = arc * swirl
        for c in range(1, channels):
            rate = (
                thin * laplace[c]
                - push * (outer[c] - inner[c])
                - turn * (ahead[c] - behind[c])
            )
            if upper is not None:
                rate = rate - drift * upper[c]
            if lower is not None:
                rate = rate + drift * lower[c]
            if c == 2:
                rate = rate + (DT * reciprocal) * swirl * swirl
            if c == 3:
                rate = rate - (DT * reciprocal) * swirl * radial
            found.append(rate)
        return thin, found

    def in_plane(step, chunk):
        to_right(step, chunk).wait_recv()
        if sectors > 2:
            to_left(step, chunk).wait_recv()
        for start in range(bounds[chunk], bounds[chunk + 1], 8):
            shape = (8, columns)
            lane = lax.broadcasted_iota(jnp.int32, shape, 1)
            weights = terms(start, shape)
            edges = edge_left[step, pl.ds(start, 8)]
            if sectors > 2:
                edges = jnp.where(lane % 2 == 0, edges, edge_right[step, pl.ds(start, 8)])

            def cell(channel, plane, offset=0):
                return state[step, channel, plane, pl.ds(PAD + start + offset, 8)]

            def cells(plane, offset=0):
                return [cell(c, plane, offset) for c in range(channels)]

            for plane in range(planes):
                center = cells(plane)
                ahead, behind = [], []
                for c in range(channels):
                    block = c * planes + plane
                    rim = pltpu.roll(edges, (columns - 2 * block - 1) % columns, 1)
                    ahead.append(
                        pltpu.roll(jnp.where(lane == 0, rim, center[c]), columns - 1, 1)
                    )
                    behind.append(
                        pltpu.roll(jnp.where(lane == columns - 1, rim, center[c]), 1, 1)
                    )
                thin, rate = plane_rates(
                    weights,
                    center,
                    cells(plane, 1),
                    cells(plane, -1),
                    ahead,
                    behind,
                    cells(plane + 1) if plane < planes - 1 else None,
                    cells(plane - 1) if plane > 0 else None,
                )
                spread[plane, pl.ds(start, 8)] = thin
                for c in range(channels):
                    increment[c, plane, pl.ds(start, 8)] = rate[c]

    def in_circle(step):
        if step == 0:
            load_circle.wait()
            for shift in range(1, sectors):
                gather(shift).wait_recv()
        else:
            receive_rim(step)
        for c in range(channels):
            sign = 1.0 if c < 2 else -1.0
            for plane in range(planes):
                first = circle[step, c, plane, pl.ds(PAD, 8)]
                circle[step, c, plane, pl.ds(PAD - 1, 1)] = (
                    sign * pltpu.roll(first, around // 2, 1)[:1]
                )
        for start in range(0, rings, 8):
            weights = terms(start, (8, around))

            def cells(plane, offset=0):
                return [
                    circle[step, c, plane, pl.ds(PAD + start + offset, 8)]
                    for c in range(channels)
                ]

            for plane in range(planes):
                center = cells(plane)
                thin, rate = plane_rates(
                    weights,
                    center,
                    cells(plane, 1),
                    cells(plane, -1),
                    [pltpu.roll(x, around - 1, 1) for x in center],
                    [pltpu.roll(x, 1, 1) for x in center],
                    cells(plane + 1) if plane < planes - 1 else None,
                    cells(plane - 1) if plane > 0 else None,
                )
                circle_spread[plane, pl.ds(start, 8)] = thin
                for c in range(channels):
                    circle_increment[c, plane, pl.ds(start, 8)] = rate[c]

    def receive_planes(step, chunk):
        @pl.when(has_low)
        def _():
            to_high(step, chunk).wait_recv()

        @pl.when(has_high)
        def _():
            to_low(step, chunk).wait_recv()

    def add_planes(step, chunk):
        for plane, halo, sign in ((0, low_plane, 1.0), (planes - 1, high_plane, -1.0)):
            here = span(chunk)
            drift = (sign * 0.5 * DT) * state[step, 1, plane, own(chunk)]
            weight = drift + spread[plane, here]
            level = halo[step, 0, here]
            increment[0, plane, here] += level * (
                DT * KAPPA + (sign * 0.5 * DT) * halo[step, 1, here]
            )
            for c in range(1, channels):
                increment[c, plane, here] += weight * halo[step, c, here]

    def store(step, chunk):
        for c in range(channels):
            for plane in range(planes):
                value = state[step, c, plane, own(chunk)] + increment[c, plane, span(chunk)]
                if step == STEPS - 1:
                    out_ref[c, plane, span(chunk)] = value
                else:
                    state[step + 1, c, plane, own(chunk)] = value

    def add_circle(step):
        for plane, halo, sign in ((0, circle_low, 1.0), (planes - 1, circle_high, -1.0)):
            drift = (sign * 0.5 * DT) * circle[step, 1, plane, pl.ds(PAD, rings)]
            weight = drift + circle_spread[plane]
            circle_increment[0, plane] += halo[step, 0] * (
                DT * KAPPA + (sign * 0.5 * DT) * halo[step, 1]
            )
            for c in range(1, channels):
                circle_increment[c, plane] += weight * halo[step, c]

    level_count = columns.bit_length() - 1

    def make_basis():
        for level in range(level_count):
            width = 2 << level
            shape = (2 * columns, columns)
            row = lax.broadcasted_iota(jnp.int32, shape, 0) % columns
            lane = lax.broadcasted_iota(jnp.int32, shape, 1)
            same = jnp.where(row // width == lane // width, 1.0 / width, 0.0)
            basis[:, pl.ds(level * columns, columns)] = same.astype(jnp.bfloat16)

    def block_means(step):
        shape = (8, columns)
        row = lax.broadcasted_iota(jnp.int32, shape, 0)
        for start in range(0, rings, 8):
            width = jnp.zeros(shape, jnp.int32)
            for ring in range(8):
                width = jnp.where(row == ring, width_smem[start + ring], width)
            values = jnp.concatenate(
                [
                    circle_increment[
                        block // planes,
                        block % planes,
                        pl.ds(start, 8),
                        pl.ds(sector * columns, columns),
                    ]
                    for block in range(blocks)
                    for sector in range(sectors)
                ],
                axis=0,
            )
            coarse = values.astype(jnp.bfloat16)
            fine = (values - coarse.astype(jnp.float32)).astype(jnp.bfloat16)
            means = jnp.dot(
                jnp.concatenate([coarse, fine], axis=1),
                basis[...],
                preferred_element_type=jnp.float32,
            )
            for block in range(blocks):
                picked, whole = [], []
                for sector in range(sectors):
                    first = (block * sectors + sector) * 8
                    mean = None
                    for level in range(level_count):
                        part = means[
                            first : first + 8, level * columns : (level + 1) * columns
                        ]
                        if mean is None:
                            mean = part
                        else:
                            mean = jnp.where(width == 2 << level, part, mean)
                    whole.append(part)
                    picked.append(mean)
                size = 2
                while size <= sectors:
                    for sector in range(sectors):
                        total = jnp.zeros(shape, jnp.float32)
                        for other in range(sectors):
                            if size == sectors:
                                total = total + whole[other]
                            else:
                                same = (az + sector) % sectors // size == (
                                    az + other
                                ) % sectors // size
                                total = total + jnp.where(same, 1.0, 0.0) * whole[other]
                        picked[sector] = jnp.where(
                            width == size * columns, total * (1.0 / size), picked[sector]
                        )
                    size *= 2
                c, plane = block // planes, block % planes
                here = pl.ds(PAD + start, 8)
                for sector in range(sectors):
                    lanes = pl.ds(sector * columns, columns)
                    if step == STEPS - 1 and sector > 0:
                        continue
                    value = circle[step, c, plane, here, lanes] + picked[sector]
                    if step == STEPS - 1:
                        out_ref[c, plane, pl.ds(start, 8)] = value
                    else:
                        circle[step + 1, c, plane, here, lanes] = value
                        if sector == 0:
                            state[step + 1, c, plane, here] = value

    off_axis = jnp.logical_not(at_axis)

    @pl.when(at_axis)
    def _():
        send_circle(0)
        for shift in range(1, sectors):
            gather(shift).start()

    @pl.when(off_axis)
    def _():
        send_planes(0, 0)

    for chunk in range(1, chunks):
        send_planes(0, chunk)

    @pl.when(jnp.logical_not(has_low))
    def _():
        low_plane[...] = jnp.zeros(low_plane.shape, jnp.float32)
        circle_low[...] = jnp.zeros(circle_low.shape, jnp.float32)

    @pl.when(jnp.logical_not(has_high))
    def _():
        high_plane[...] = jnp.zeros(high_plane.shape, jnp.float32)
        circle_high[...] = jnp.zeros(circle_high.shape, jnp.float32)

    load.wait()
    send_last_row(0)

    @pl.when(off_axis)
    def _():
        send_first_row(0)
        send_edges(0, 0)

    for chunk in range(1, chunks):
        send_edges(0, chunk)

    @pl.when(at_axis)
    def _():
        make_basis()

    load_width.wait()
    for step in range(STEPS):
        last = step == STEPS - 1
        receive_rows(step)

        @pl.when(at_axis)
        def _():
            in_circle(step)

        @pl.when(off_axis)
        def _():
            in_plane(step, 0)

        for chunk in range(1, chunks):
            in_plane(step, chunk)

        @pl.when(off_axis)
        def _():
            receive_planes(step, 0)
            add_planes(step, 0)
            store(step, 0)
            if not last:
                send_planes(step + 1, 0)
                send_edges(step + 1, 0)
                send_first_row(step + 1)

        for chunk in range(1, chunks):
            receive_planes(step, chunk)
            add_planes(step, chunk)
            store(step, chunk)
            if not last:
                send_planes(step + 1, chunk)
                send_edges(step + 1, chunk)
                if chunk == 1:

                    @pl.when(at_axis)
                    def _():
                        send_rim(step + 1)

                if chunk == chunks - 1:
                    send_last_row(step + 1)

        @pl.when(at_axis)
        def _():
            receive_circle(step)
            add_circle(step)
            block_means(step)
            if not last:
                send_circle(step + 1)

    @pl.when(off_axis)
    def _():
        load_circle.wait()

    for step in range(STEPS):
        for chunk in range(chunks):

            def sent():
                @pl.when(has_low)
                def _():
                    to_low(step, chunk).wait_send()

                @pl.when(has_high)
                def _():
                    to_high(step, chunk).wait_send()

                to_right(step, chunk).wait_send()
                if sectors > 2:
                    to_left(step, chunk).wait_send()

            if chunk == 0:
                pl.when(off_axis)(sent)
            else:
                sent()

        @pl.when(has_inner)
        def _():
            to_inner(step).wait_send()

        @pl.when(has_outer)
        def _():
            to_outer(step).wait_send()

        @pl.when(at_axis)
        def _():
            @pl.when(has_low)
            def _():
                circle_to_low(step).wait_send()
                if step == 0:
                    for shift in range(1, sectors):
                        corner_to_low(shift).wait_send()

            @pl.when(has_high)
            def _():
                circle_to_high(step).wait_send()
                if step == 0:
                    for shift in range(1, sectors):
                        corner_to_high(shift).wait_send()

            for shift in range(1, sectors):
                if step == 0:
                    gather(shift).wait_send()
                else:
                    to_rim(step, shift).wait_send()


def local(sizes, flow_state, cycle_widths):
    channels, planes, rows, columns = flow_state.shape
    rings = cycle_widths.shape[0]
    sectors = sizes[1]
    middle = rings + ((rows - rings) // 2 + 7) // 8 * 8
    bounds = (0, rings, middle, rows)
    chunks = len(bounds) - 1
    blocks = channels * planes
    around = sectors * columns
    f32 = jnp.float32
    dma = pltpu.SemaphoreType.DMA
    return pl.pallas_call(
        functools.partial(kernel, sizes, bounds),
        out_shape=pltpu.VMEM(flow_state.shape, f32),
        in_specs=[
            pl.BlockSpec(memory_space=pl.ANY),
            pl.BlockSpec(memory_space=pl.ANY),
        ],
        out_specs=pl.BlockSpec(memory_space=pltpu.VMEM),
        scratch_shapes=[
            pltpu.VMEM((STEPS, channels, planes, rows + 2 * PAD, columns), f32),
            pltpu.VMEM((channels, planes, rows, columns), f32),
            pltpu.VMEM((planes, rows, columns), f32),
            pltpu.VMEM((STEPS, channels, rows, columns), f32),
            pltpu.VMEM((STEPS, channels, rows, columns), f32),
            pltpu.VMEM((STEPS, rows, columns), f32),
            pltpu.VMEM((STEPS, rows, columns), f32),
            pltpu.VMEM((STEPS, rows, columns), f32),
            pltpu.VMEM((STEPS, 2, blocks, columns), f32),
            pltpu.VMEM((STEPS, 2, blocks, columns), f32),
            pltpu.VMEM((STEPS, channels, planes, rings + 2 * PAD, around), f32),
            pltpu.VMEM((channels, planes, rings, around), f32),
            pltpu.VMEM((planes, rings, around), f32),
            pltpu.VMEM((STEPS, channels, rings, around), f32),
            pltpu.VMEM((STEPS, channels, rings, around), f32),
            pltpu.VMEM((STEPS, sectors - 1, blocks, columns), f32),
            pltpu.VMEM((2 * columns, (columns.bit_length() - 1) * columns), jnp.bfloat16),
            pltpu.SMEM((rings,), jnp.int32),
            dma,
            dma,
            dma,
            dma((STEPS, chunks)),
            dma((STEPS, chunks)),
            dma((STEPS, chunks)),
            dma((STEPS, chunks)),
            dma((STEPS, chunks)),
            dma((STEPS, chunks)),
            dma((STEPS, chunks)),
            dma((STEPS, chunks)),
            dma((STEPS, 2)),
            dma((STEPS, 2)),
            dma((sectors - 1,)),
            dma((sectors - 1,)),
            dma((sectors - 1,)),
            dma((sectors - 1,)),
            dma((sectors - 1,)),
            dma((sectors - 1,)),
            dma((STEPS, sectors - 1)),
            dma((STEPS, sectors - 1)),
        ],
        compiler_params=pltpu.CompilerParams(
            collective_id=0, has_side_effects=True, vmem_limit_bytes=64 * 1024 * 1024 - 262144
        ),
    )(flow_state, cycle_widths)


def solution(mesh):
    sizes = (mesh.shape["ax"], mesh.shape["az"], mesh.shape["rad"])
    return jax.shard_map(
        functools.partial(local, sizes),
        mesh=mesh,
        in_specs=(P(None, ("groups", "ax"), "rad", "az"), P()),
        out_specs=P(None, ("groups", "ax"), "rad", "az"),
        check_vma=False,
    )
```

```python
import functools
import math

import jax
import jax.numpy as jnp
from jax import lax
from jax.experimental import pallas as pl
from jax.experimental.pallas import tpu as pltpu
from jax.sharding import PartitionSpec as P

STEPS = 2
DT = 0.2
KAPPA = 0.05
VISC = 0.1
RHO_RATIO = 20.0
PAD = 8
MESH = pl.DeviceIdType.MESH


def kernel(
    sizes,
    bounds,
    flow_ref,
    width_ref,
    out_ref,
    state,
    increment,
    spread,
    low_plane,
    high_plane,
    edge_out,
    edge_left,
    edge_right,
    row_out,
    row_in,
    circle,
    circle_increment,
    circle_spread,
    circle_low,
    circle_high,
    rim_in,
    basis,
    width_smem,
    load_sem,
    width_sem,
    circle_sem,
    low_send,
    low_recv,
    high_send,
    high_recv,
    left_send,
    left_recv,
    right_send,
    right_recv,
    row_send,
    row_recv,
    gather_send,
    gather_recv,
    corner_low_send,
    corner_low_recv,
    corner_high_send,
    corner_high_recv,
    rim_send,
    rim_recv,
):
    axials, sectors, rads = sizes
    channels, planes, rows, columns = flow_ref.shape
    blocks = channels * planes
    rings = width_ref.shape[0]
    around = sectors * columns
    chunks = len(bounds) - 1
    ax = lax.axis_index("ax")
    az = lax.axis_index("az")
    rad = lax.axis_index("rad")
    angle_step = 2.0 * math.pi / (sectors * columns)
    half_arc = DT / (2.0 * angle_step)
    has_low = ax > 0
    has_high = ax < axials - 1
    has_inner = rad > 0
    has_outer = rad < rads - 1
    at_axis = rad == 0
    left = (az + sectors - 1) % sectors
    right = (az + 1) % sectors

    load = pltpu.make_async_copy(
        flow_ref, state.at[0, :, :, pl.ds(PAD, rows)], load_sem
    )
    load.start()
    load_width = pltpu.make_async_copy(width_ref, width_smem, width_sem)
    load_width.start()
    load_circle = pltpu.make_async_copy(
        flow_ref.at[:, :, pl.ds(0, rings + 8)],
        circle.at[0, :, :, pl.ds(PAD, rings + 8), pl.ds(0, columns)],
        circle_sem,
    )
    load_circle.start()

    barrier = pltpu.get_barrier_semaphore()

    def greet(axis, place):
        pl.semaphore_signal(barrier, inc=1, device_id={axis: place}, device_id_type=MESH)

    def greet_corner(place, shift):
        pl.semaphore_signal(
            barrier,
            inc=1,
            device_id={"ax": place, "az": (az + shift) % sectors},
            device_id_type=MESH,
        )

    @pl.when(has_low)
    def _():
        greet("ax", ax - 1)

    @pl.when(has_high)
    def _():
        greet("ax", ax + 1)

    @pl.when(has_inner)
    def _():
        greet("rad", rad - 1)

    @pl.when(has_outer)
    def _():
        greet("rad", rad + 1)

    for shift in range(1, sectors):
        greet("az", (az + shift) % sectors)

    @pl.when(jnp.logical_and(at_axis, has_low))
    def _():
        for shift in range(1, sectors):
            greet_corner(ax - 1, shift)

    @pl.when(jnp.logical_and(at_axis, has_high))
    def _():
        for shift in range(1, sectors):
            greet_corner(ax + 1, shift)

    def one(flag):
        return jnp.where(flag, 1, 0)

    pl.semaphore_wait(
        barrier,
        one(has_low)
        + one(has_high)
        + one(has_inner)
        + one(has_outer)
        + sectors
        - 1
        + one(at_axis) * (one(has_low) + one(has_high)) * (sectors - 1),
    )

    def remote(src, dst, send, recv, axis, place):
        return pltpu.make_async_remote_copy(
            src_ref=src,
            dst_ref=dst,
            send_sem=send,
            recv_sem=recv,
            device_id={axis: place},
            device_id_type=MESH,
        )

    def span(chunk):
        return pl.ds(bounds[chunk], bounds[chunk + 1] - bounds[chunk])

    def own(chunk):
        return pl.ds(PAD + bounds[chunk], bounds[chunk + 1] - bounds[chunk])

    def source(step, plane, chunk):
        if step == 0:
            return flow_ref.at[:, plane, span(chunk)]
        return state.at[step, :, plane, own(chunk)]

    def to_low(step, chunk):
        return remote(
            source(step, 0, chunk),
            high_plane.at[step, :, span(chunk)],
            low_send.at[step, chunk],
            low_recv.at[step, chunk],
            "ax",
            ax - 1,
        )

    def to_high(step, chunk):
        return remote(
            source(step, planes - 1, chunk),
            low_plane.at[step, :, span(chunk)],
            high_send.at[step, chunk],
            high_recv.at[step, chunk],
            "ax",
            ax + 1,
        )

    def to_right(step, chunk):
        return remote(
            edge_out.at[step, span(chunk)],
            edge_left.at[step, span(chunk)],
            right_send.at[step, chunk],
            right_recv.at[step, chunk],
            "az",
            right,
        )

    def to_left(step, chunk):
        return remote(
            edge_out.at[step, span(chunk)],
            edge_right.at[step, span(chunk)],
            left_send.at[step, chunk],
            left_recv.at[step, chunk],
            "az",
            left,
        )

    def to_inner(step):
        return remote(
            row_out.at[step, 0],
            row_in.at[step, 1],
            row_send.at[step, 0],
            row_recv.at[step, 0],
            "rad",
            rad - 1,
        )

    def to_outer(step):
        return remote(
            row_out.at[step, 1],
            row_in.at[step, 0],
            row_send.at[step, 1],
            row_recv.at[step, 1],
            "rad",
            rad + 1,
        )

    def circle_source(step, plane):
        if step == 0:
            return flow_ref.at[:, plane, pl.ds(0, rings)]
        return circle.at[step, :, plane, pl.ds(PAD, rings)]

    def circle_target(ref, step):
        if step == 0:
            return ref.at[step, :, :, pl.ds(0, columns)]
        return ref.at[step]

    def circle_to_low(step):
        return remote(
            circle_source(step, 0),
            circle_target(circle_high, step),
            low_send.at[step, 0],
            low_recv.at[step, 0],
            "ax",
            ax - 1,
        )

    def circle_to_high(step):
        return remote(
            circle_source(step, planes - 1),
            circle_target(circle_low, step),
            high_send.at[step, 0],
            high_recv.at[step, 0],
            "ax",
            ax + 1,
        )

    def corner_to_low(shift):
        return pltpu.make_async_remote_copy(
            src_ref=flow_ref.at[:, 0, pl.ds(0, rings)],
            dst_ref=circle_high.at[0, :, :, pl.ds((sectors - shift) * columns, columns)],
            send_sem=corner_low_send.at[shift - 1],
            recv_sem=corner_low_recv.at[shift - 1],
            device_id={"ax": ax - 1, "az": (az + shift) % sectors},
            device_id_type=MESH,
        )

    def corner_to_high(shift):
        return pltpu.make_async_remote_copy(
            src_ref=flow_ref.at[:, planes - 1, pl.ds(0, rings)],
            dst_ref=circle_low.at[0, :, :, pl.ds((sectors - shift) * columns, columns)],
            send_sem=corner_high_send.at[shift - 1],
            recv_sem=corner_high_recv.at[shift - 1],
            device_id={"ax": ax + 1, "az": (az + shift) % sectors},
            device_id_type=MESH,
        )

    def gather(shift):
        return remote(
            flow_ref.at[:, :, pl.ds(0, rings + 8)],
            circle.at[
                0, :, :, pl.ds(PAD, rings + 8), pl.ds((sectors - shift) * columns, columns)
            ],
            gather_send.at[shift - 1],
            gather_recv.at[shift - 1],
            "az",
            (az + shift) % sectors,
        )

    def to_rim(step, shift):
        return remote(
            row_out.at[step, 0],
            rim_in.at[step, sectors - shift - 1],
            rim_send.at[step, shift - 1],
            rim_recv.at[step, shift - 1],
            "az",
            (az + shift) % sectors,
        )

    def send_circle(step):
        @pl.when(has_low)
        def _():
            circle_to_low(step).start()
            if step == 0:
                for shift in range(1, sectors):
                    corner_to_low(shift).start()

        @pl.when(has_high)
        def _():
            circle_to_high(step).start()
            if step == 0:
                for shift in range(1, sectors):
                    corner_to_high(shift).start()

    def receive_circle(step):
        @pl.when(has_low)
        def _():
            circle_to_high(step).wait_recv()
            if step == 0:
                for shift in range(1, sectors):
                    corner_to_high(shift).wait_recv()

        @pl.when(has_high)
        def _():
            circle_to_low(step).wait_recv()
            if step == 0:
                for shift in range(1, sectors):
                    corner_to_low(shift).wait_recv()

    def send_rim(step):
        for block in range(blocks):
            row = state[step, block // planes, block % planes, pl.ds(PAD + rings, 1)]
            row_out[step, 0, pl.ds(block, 1)] = row
            circle[
                step, block // planes, block % planes, pl.ds(PAD + rings, 1), pl.ds(0, columns)
            ] = row
        for shift in range(1, sectors):
            to_rim(step, shift).start()

    def receive_rim(step):
        for shift in range(1, sectors):
            to_rim(step, shift).wait_recv()
            place = sectors - shift
            for block in range(blocks):
                circle[
                    step,
                    block // planes,
                    block % planes,
                    pl.ds(PAD + rings, 1),
                    pl.ds(place * columns, columns),
                ] = rim_in[step, place - 1, pl.ds(block, 1)]

    def send_planes(step, chunk):
        @pl.when(has_low)
        def _():
            to_low(step, chunk).start()

        @pl.when(has_high)
        def _():
            to_high(step, chunk).start()

    def send_edges(step, chunk):
        count = bounds[chunk + 1] - bounds[chunk]
        lane = lax.broadcasted_iota(jnp.int32, (count, columns), 1)
        packed = jnp.zeros((count, columns), jnp.float32)
        for block in range(blocks):
            values = state[step, block // planes, block % planes, own(chunk)]
            packed = jnp.where(
                lane // 2 == block, pltpu.roll(values, 2 * block + 1, 1), packed
            )
        edge_out[step, span(chunk)] = packed
        to_right(step, chunk).start()
        if sectors > 2:
            to_left(step, chunk).start()

    def send_first_row(step):
        for block in range(blocks):
            row_out[step, 0, pl.ds(block, 1)] = state[
                step, block // planes, block % planes, pl.ds(PAD, 1)
            ]

        to_inner(step).start()

    def send_last_row(step):
        for block in range(blocks):
            row_out[step, 1, pl.ds(block, 1)] = state[
                step, block // planes, block % planes, pl.ds(PAD + rows - 1, 1)
            ]

        @pl.when(has_outer)
        def _():
            to_outer(step).start()

    def receive_rows(step):
        @pl.when(has_inner)
        def _():
            to_outer(step).wait_recv()
            for block in range(blocks):
                state[step, block // planes, block % planes, pl.ds(PAD - 1, 1)] = row_in[
                    step, 0, pl.ds(block, 1)
                ]

        @pl.when(has_outer)
        def _():
            to_inner(step).wait_recv()
            for block in range(blocks):
                state[step, block // planes, block % planes, pl.ds(PAD + rows, 1)] = row_in[
                    step, 1, pl.ds(block, 1)
                ]

        @pl.when(jnp.logical_not(has_outer))
        def _():
            for block in range(blocks):
                state[step, block // planes, block % planes, pl.ds(PAD + rows, 1)] = jnp.zeros(
                    (1, columns), jnp.float32
                )

    def terms(start, shape):
        row = lax.broadcasted_iota(jnp.int32, shape, 0)
        radius = (rad * rows + start + row).astype(jnp.float32) + 0.5
        reciprocal = 1.0 / radius
        return (
            reciprocal,
            half_arc * reciprocal,
            1.0 + 0.5 * reciprocal,
            1.0 - 0.5 * reciprocal,
            (0.5 * DT) * (1.0 + reciprocal),
            (0.5 * DT) * (1.0 - reciprocal),
        )

    def plane_rates(weights, center, outer, inner, ahead, behind, upper, lower):
        reciprocal, arc, outer_weight, inner_weight, outer_flux, inner_flux = weights
        level, axial, radial, swirl = center
        density = 1.0 + (RHO_RATIO - 1.0) * jnp.clip(level, 0.0, 1.0)
        thin = (DT * VISC) / density
        laplace = [
            outer_weight * outer[c] + inner_weight * inner[c] - 4.0 * center[c]
            for c in range(channels)
        ]
        for other in (upper, lower):
            if other is not None:
                laplace = [laplace[c] + other[c] for c in range(channels)]
        rate = (
            (DT * KAPPA) * laplace[0]
            - outer_flux * outer[2] * outer[0]
            + inner_flux * inner[2] * inner[0]
            - arc * (ahead[3] * ahead[0] - behind[3] * behind[0])
        )
        if upper is not None:
            rate = rate - (0.5 * DT) * upper[1] * upper[0]
        if lower is not None:
            rate = rate + (0.5 * DT) * lower[1] * lower[0]
        found = [rate]
        drift = (0.5 * DT) * axial
        push = (0.5 * DT) * radial
        turn = arc * swirl
        for c in range(1, channels):
            rate = (
                thin * laplace[c]
                - push * (outer[c] - inner[c])
                - turn * (ahead[c] - behind[c])
            )
            if upper is not None:
                rate = rate - drift * upper[c]
            if lower is not None:
                rate = rate + drift * lower[c]
            if c == 2:
                rate = rate + (DT * reciprocal) * swirl * swirl
            if c == 3:
                rate = rate - (DT * reciprocal) * swirl * radial
            found.append(rate)
        return thin, found

    def in_plane(step, chunk):
        to_right(step, chunk).wait_recv()
        if sectors > 2:
            to_left(step, chunk).wait_recv()
        for start in range(bounds[chunk], bounds[chunk + 1], 8):
            shape = (8, columns)
            lane = lax.broadcasted_iota(jnp.int32, shape, 1)
            weights = terms(start, shape)
            edges = edge_left[step, pl.ds(start, 8)]
            if sectors > 2:
                edges = jnp.where(lane % 2 == 0, edges, edge_right[step, pl.ds(start, 8)])

            def cell(channel, plane, offset=0):
                return state[step, channel, plane, pl.ds(PAD + start + offset, 8)]

            def cells(plane, offset=0):
                return [cell(c, plane, offset) for c in range(channels)]

            for plane in range(planes):
                center = cells(plane)
                ahead, behind = [], []
                for c in range(channels):
                    block = c * planes + plane
                    rim = pltpu.roll(edges, (columns - 2 * block - 1) % columns, 1)
                    ahead.append(
                        pltpu.roll(jnp.where(lane == 0, rim, center[c]), columns - 1, 1)
                    )
                    behind.append(
                        pltpu.roll(jnp.where(lane == columns - 1, rim, center[c]), 1, 1)
                    )
                thin, rate = plane_rates(
                    weights,
                    center,
                    cells(plane, 1),
                    cells(plane, -1),
                    ahead,
                    behind,
                    cells(plane + 1) if plane < planes - 1 else None,
                    cells(plane - 1) if plane > 0 else None,
                )
                spread[plane, pl.ds(start, 8)] = thin
                for c in range(channels):
                    increment[c, plane, pl.ds(start, 8)] = rate[c]

    def in_circle(step):
        if step == 0:
            load_circle.wait()
            for shift in range(1, sectors):
                gather(shift).wait_recv()
        else:
            receive_rim(step)
        for c in range(channels):
            sign = 1.0 if c < 2 else -1.0
            for plane in range(planes):
                first = circle[step, c, plane, pl.ds(PAD, 8)]
                circle[step, c, plane, pl.ds(PAD - 1, 1)] = (
                    sign * pltpu.roll(first, around // 2, 1)[:1]
                )
        for start in range(0, rings, 8):
            weights = terms(start, (8, around))

            def cells(plane, offset=0):
                return [
                    circle[step, c, plane, pl.ds(PAD + start + offset, 8)]
                    for c in range(channels)
                ]

            for plane in range(planes):
                center = cells(plane)
                thin, rate = plane_rates(
                    weights,
                    center,
                    cells(plane, 1),
                    cells(plane, -1),
                    [pltpu.roll(x, around - 1, 1) for x in center],
                    [pltpu.roll(x, 1, 1) for x in center],
                    cells(plane + 1) if plane < planes - 1 else None,
                    cells(plane - 1) if plane > 0 else None,
                )
                circle_spread[plane, pl.ds(start, 8)] = thin
                for c in range(channels):
                    circle_increment[c, plane, pl.ds(start, 8)] = rate[c]

    def receive_planes(step, chunk):
        @pl.when(has_low)
        def _():
            to_high(step, chunk).wait_recv()

        @pl.when(has_high)
        def _():
            to_low(step, chunk).wait_recv()

    def add_planes(step, chunk):
        for plane, halo, sign in ((0, low_plane, 1.0), (planes - 1, high_plane, -1.0)):
            here = span(chunk)
            drift = (sign * 0.5 * DT) * state[step, 1, plane, own(chunk)]
            weight = drift + spread[plane, here]
            level = halo[step, 0, here]
            increment[0, plane, here] += level * (
                DT * KAPPA + (sign * 0.5 * DT) * halo[step, 1, here]
            )
            for c in range(1, channels):
                increment[c, plane, here] += weight * halo[step, c, here]

    def store(step, chunk):
        for c in range(channels):
            for plane in range(planes):
                value = state[step, c, plane, own(chunk)] + increment[c, plane, span(chunk)]
                if step == STEPS - 1:
                    out_ref[c, plane, span(chunk)] = value
                else:
                    state[step + 1, c, plane, own(chunk)] = value

    def add_circle(step):
        for plane, halo, sign in ((0, circle_low, 1.0), (planes - 1, circle_high, -1.0)):
            drift = (sign * 0.5 * DT) * circle[step, 1, plane, pl.ds(PAD, rings)]
            weight = drift + circle_spread[plane]
            circle_increment[0, plane] += halo[step, 0] * (
                DT * KAPPA + (sign * 0.5 * DT) * halo[step, 1]
            )
            for c in range(1, channels):
                circle_increment[c, plane] += weight * halo[step, c]

    level_count = columns.bit_length() - 1

    def make_basis():
        for level in range(level_count):
            width = 2 << level
            shape = (2 * columns, columns)
            row = lax.broadcasted_iota(jnp.int32, shape, 0) % columns
            lane = lax.broadcasted_iota(jnp.int32, shape, 1)
            same = jnp.where(row // width == lane // width, 1.0 / width, 0.0)
            basis[:, pl.ds(level * columns, columns)] = same.astype(jnp.bfloat16)

    def block_means(step):
        shape = (8, columns)
        row = lax.broadcasted_iota(jnp.int32, shape, 0)
        for start in range(0, rings, 8):
            width = jnp.zeros(shape, jnp.int32)
            for ring in range(8):
                width = jnp.where(row == ring, width_smem[start + ring], width)
            values = jnp.concatenate(
                [
                    circle_increment[
                        block // planes,
                        block % planes,
                        pl.ds(start, 8),
                        pl.ds(sector * columns, columns),
                    ]
                    for block in range(blocks)
                    for sector in range(sectors)
                ],
                axis=0,
            )
            coarse = values.astype(jnp.bfloat16)
            fine = (values - coarse.astype(jnp.float32)).astype(jnp.bfloat16)
            means = jnp.dot(
                jnp.concatenate([coarse, fine], axis=1),
                basis[...],
                preferred_element_type=jnp.float32,
            )
            for block in range(blocks):
                picked, whole = [], []
                for sector in range(sectors):
                    first = (block * sectors + sector) * 8
                    mean = None
                    for level in range(level_count):
                        part = means[
                            first : first + 8, level * columns : (level + 1) * columns
                        ]
                        if mean is None:
                            mean = part
                        else:
                            mean = jnp.where(width == 2 << level, part, mean)
                    whole.append(part)
                    picked.append(mean)
                size = 2
                while size <= sectors:
                    for sector in range(sectors):
                        total = jnp.zeros(shape, jnp.float32)
                        for other in range(sectors):
                            if size == sectors:
                                total = total + whole[other]
                            else:
                                same = (az + sector) % sectors // size == (
                                    az + other
                                ) % sectors // size
                                total = total + jnp.where(same, 1.0, 0.0) * whole[other]
                        picked[sector] = jnp.where(
                            width == size * columns, total * (1.0 / size), picked[sector]
                        )
                    size *= 2
                c, plane = block // planes, block % planes
                here = pl.ds(PAD + start, 8)
                for sector in range(sectors):
                    lanes = pl.ds(sector * columns, columns)
                    if step == STEPS - 1 and sector > 0:
                        continue
                    value = circle[step, c, plane, here, lanes] + picked[sector]
                    if step == STEPS - 1:
                        out_ref[c, plane, pl.ds(start, 8)] = value
                    else:
                        circle[step + 1, c, plane, here, lanes] = value
                        if sector == 0:
                            state[step + 1, c, plane, here] = value

    off_axis = jnp.logical_not(at_axis)

    @pl.when(at_axis)
    def _():
        send_circle(0)
        for shift in range(1, sectors):
            gather(shift).start()

    @pl.when(off_axis)
    def _():
        send_planes(0, 0)

    for chunk in range(1, chunks):
        send_planes(0, chunk)

    @pl.when(jnp.logical_not(has_low))
    def _():
        low_plane[...] = jnp.zeros(low_plane.shape, jnp.float32)
        circle_low[...] = jnp.zeros(circle_low.shape, jnp.float32)

    @pl.when(jnp.logical_not(has_high))
    def _():
        high_plane[...] = jnp.zeros(high_plane.shape, jnp.float32)
        circle_high[...] = jnp.zeros(circle_high.shape, jnp.float32)

    load.wait()
    send_last_row(0)

    @pl.when(off_axis)
    def _():
        send_first_row(0)
        send_edges(0, 0)

    for chunk in range(1, chunks):
        send_edges(0, chunk)

    @pl.when(at_axis)
    def _():
        make_basis()

    load_width.wait()
    for step in range(STEPS):
        last = step == STEPS - 1

        @pl.when(at_axis)
        def _():
            in_circle(step)
            receive_circle(step)
            add_circle(step)
            block_means(step)
            if not last:
                send_circle(step + 1)

        receive_rows(step)

        @pl.when(off_axis)
        def _():
            in_plane(step, 0)

        for chunk in range(1, chunks):
            in_plane(step, chunk)

        @pl.when(off_axis)
        def _():
            receive_planes(step, 0)
            add_planes(step, 0)
            store(step, 0)
            if not last:
                send_planes(step + 1, 0)
                send_edges(step + 1, 0)
                send_first_row(step + 1)

        for chunk in range(1, chunks):
            receive_planes(step, chunk)
            add_planes(step, chunk)
            store(step, chunk)
            if not last:
                send_planes(step + 1, chunk)
                send_edges(step + 1, chunk)
                if chunk == 1:

                    @pl.when(at_axis)
                    def _():
                        send_rim(step + 1)

                if chunk == chunks - 1:
                    send_last_row(step + 1)

    @pl.when(off_axis)
    def _():
        load_circle.wait()

    for step in range(STEPS):
        for chunk in range(chunks):

            def sent():
                @pl.when(has_low)
                def _():
                    to_low(step, chunk).wait_send()

                @pl.when(has_high)
                def _():
                    to_high(step, chunk).wait_send()

                to_right(step, chunk).wait_send()
                if sectors > 2:
                    to_left(step, chunk).wait_send()

            if chunk == 0:
                pl.when(off_axis)(sent)
            else:
                sent()

        @pl.when(has_inner)
        def _():
            to_inner(step).wait_send()

        @pl.when(has_outer)
        def _():
            to_outer(step).wait_send()

        @pl.when(at_axis)
        def _():
            @pl.when(has_low)
            def _():
                circle_to_low(step).wait_send()
                if step == 0:
                    for shift in range(1, sectors):
                        corner_to_low(shift).wait_send()

            @pl.when(has_high)
            def _():
                circle_to_high(step).wait_send()
                if step == 0:
                    for shift in range(1, sectors):
                        corner_to_high(shift).wait_send()

            for shift in range(1, sectors):
                if step == 0:
                    gather(shift).wait_send()
                else:
                    to_rim(step, shift).wait_send()


def local(sizes, flow_state, cycle_widths):
    channels, planes, rows, columns = flow_state.shape
    rings = cycle_widths.shape[0]
    sectors = sizes[1]
    middle = rings + ((rows - rings) // 2 + 7) // 8 * 8
    bounds = (0, rings, middle, rows)
    chunks = len(bounds) - 1
    blocks = channels * planes
    around = sectors * columns
    f32 = jnp.float32
    dma = pltpu.SemaphoreType.DMA
    return pl.pallas_call(
        functools.partial(kernel, sizes, bounds),
        out_shape=pltpu.VMEM(flow_state.shape, f32),
        in_specs=[
            pl.BlockSpec(memory_space=pl.ANY),
            pl.BlockSpec(memory_space=pl.ANY),
        ],
        out_specs=pl.BlockSpec(memory_space=pltpu.VMEM),
        scratch_shapes=[
            pltpu.VMEM((STEPS, channels, planes, rows + 2 * PAD, columns), f32),
            pltpu.VMEM((channels, planes, rows, columns), f32),
            pltpu.VMEM((planes, rows, columns), f32),
            pltpu.VMEM((STEPS, channels, rows, columns), f32),
            pltpu.VMEM((STEPS, channels, rows, columns), f32),
            pltpu.VMEM((STEPS, rows, columns), f32),
            pltpu.VMEM((STEPS, rows, columns), f32),
            pltpu.VMEM((STEPS, rows, columns), f32),
            pltpu.VMEM((STEPS, 2, blocks, columns), f32),
            pltpu.VMEM((STEPS, 2, blocks, columns), f32),
            pltpu.VMEM((STEPS, channels, planes, rings + 2 * PAD, around), f32),
            pltpu.VMEM((channels, planes, rings, around), f32),
            pltpu.VMEM((planes, rings, around), f32),
            pltpu.VMEM((STEPS, channels, rings, around), f32),
            pltpu.VMEM((STEPS, channels, rings, around), f32),
            pltpu.VMEM((STEPS, sectors - 1, blocks, columns), f32),
            pltpu.VMEM((2 * columns, (columns.bit_length() - 1) * columns), jnp.bfloat16),
            pltpu.SMEM((rings,), jnp.int32),
            dma,
            dma,
            dma,
            dma((STEPS, chunks)),
            dma((STEPS, chunks)),
            dma((STEPS, chunks)),
            dma((STEPS, chunks)),
            dma((STEPS, chunks)),
            dma((STEPS, chunks)),
            dma((STEPS, chunks)),
            dma((STEPS, chunks)),
            dma((STEPS, 2)),
            dma((STEPS, 2)),
            dma((sectors - 1,)),
            dma((sectors - 1,)),
            dma((sectors - 1,)),
            dma((sectors - 1,)),
            dma((sectors - 1,)),
            dma((sectors - 1,)),
            dma((STEPS, sectors - 1)),
            dma((STEPS, sectors - 1)),
        ],
        compiler_params=pltpu.CompilerParams(
            collective_id=0, has_side_effects=True, vmem_limit_bytes=64 * 1024 * 1024 - 262144
        ),
    )(flow_state, cycle_widths)


def solution(mesh):
    sizes = (mesh.shape["ax"], mesh.shape["az"], mesh.shape["rad"])
    return jax.shard_map(
        functools.partial(local, sizes),
        mesh=mesh,
        in_specs=(P(None, ("groups", "ax"), "rad", "az"), P()),
        out_specs=P(None, ("groups", "ax"), "rad", "az"),
        check_vma=False,
    )
```
